128 devices in a mesh: grp: 8 (over x, core), rep: 16 (over y, z).
Axes of the slice: x: 4, y: 4, z: 4, core: 2. Of those that a mesh axis runs over, the one named last changes fastest.
Arguments:
- item_table: bfloat16 [524288, 256], P(('grp', 'rep')), may hold values from -6 to 6
- send_rows: int32 [128, 128, 32], P(('grp', 'rep')), may hold values from 0 to 4095, as said below
- send_count: int32 [128, 128], P(('grp', 'rep')), may hold values from 24 to 32, as said below
- pos_slot: int32 [131072], P(('grp', 'rep')), may hold values from 0 to 4095, as said below
- neg_slot: int32 [128, 1024], P(('grp', 'rep')), may hold values from 0 to 4095, as said below
- user_ids: int32 [131072, 8], P(('grp', 'rep')), may hold values from 0 to 8191
- user_table: bfloat16 [8192, 256], replicated, may hold values from -2.09375 to 2.09375
- item_w1: bfloat16 [256, 512], replicated, may hold values from -0.375 to 0.375
- item_w2: bfloat16 [512, 128], replicated, may hold values from -0.25 to 0.25
- user_w1: bfloat16 [256, 512], replicated, may hold values from -0.375 to 0.375
- user_w2: bfloat16 [512, 128], replicated, may hold values from -0.25 to 0.25
Outputs:
- table_grad: float32 [524288, 256], P(('grp', 'rep'))
- example_loss: float32 [131072], P(('grp', 'rep'))
The draws below stay inside these ranges and needn't reach their ends.
Inputs may be any that keep to these rules, and one draw needn't show every extreme that they name: `send_rows`: within one list (one owner, one batch owner) the 32 entries are distinct local row numbers; entries at or beyond the list's count are unused. `send_count`: some batch owner receives 32 rows from every owner. `pos_slot`: each entry names a used slot, source * 32 + j with j below that list's count, of its batch owner's receive buffer. `neg_slot`: each entry names a used slot of its batch owner's receive buffer, numbered as for pos_slot.
All inputs are finite; a program needn't handle non-finite values.
Results may differ from the reference program's by a relative error of at most 0.02.
Values may be sent and summed in bfloat16 or wider, within the bound.
A program may use at most 128 MiB of HBM per device.

```python
import jax
import jax.numpy as jnp
from jax import lax

E = 256
H = 512
OUTW = 128
UVOCAB = 8192
FEAT = 8
ROWS_DEV = 4096
CAP = 32
B_DEV = 1024
NEG = 1024
PEERS = 128
BATCH = 131072
TROWS = 524288
N_GRP = 8
N_REP = 16


def count_table(key):
    key = jax.random.fold_in(key, 11)
    drawn = jax.random.randint(key, (PEERS, PEERS), CAP - CAP // 4, CAP + 1)
    hot_peer = jax.random.randint(jax.random.fold_in(key, 1), (), 0, PEERS)
    target_ids = jnp.arange(PEERS, dtype=jnp.int32)[None, :]
    return jnp.where(target_ids == hot_peer, CAP, drawn).astype(jnp.int32)


def used_slots(key, counts, number):
    incoming = counts.T
    end_points = jnp.cumsum(incoming, axis=1)
    totals = end_points[:, -1]
    picked_at = jax.random.randint(key, (PEERS, number), 0, totals[:, None])
    picked_at = picked_at.at[:, 0].set(totals - 1).at[:, 1].set(0)
    source = jnp.sum((end_points[:, None, :] <= picked_at[:, :, None]).astype(jnp.int32), axis=2)
    start_points = jnp.take_along_axis(end_points - incoming, source, axis=1)
    return (source * CAP + picked_at - start_points).astype(jnp.int32)


def draw_send_count(key, part):
    return count_table(key)


def draw_pos_slot(key, part):
    counts = count_table(key)
    key = jax.random.fold_in(key, 3)
    return used_slots(key, counts, B_DEV).reshape(-1)


def draw_neg_slot(key, part):
    counts = count_table(key)
    key = jax.random.fold_in(key, 5)
    return used_slots(key, counts, NEG)


def draw_send_rows(key, part):
    key = jax.random.fold_in(key, 7)
    first_row = jax.random.randint(key, (PEERS, PEERS, 1), 0, ROWS_DEV)
    first_row = first_row.at[0, 0, 0].set(ROWS_DEV - 1).at[0, 1, 0].set(0)
    stride = jax.random.randint(jax.random.fold_in(key, 1), (PEERS, PEERS, 1), 1, ROWS_DEV // CAP + 1)
    steps_along = jnp.arange(CAP, dtype=jnp.int32)[None, None, :]
    return ((first_row + steps_along * stride) % ROWS_DEV).astype(jnp.int32)


def plant(values, rng, low, high):
    longest = values.shape.index(max(values.shape))
    spots = []
    for shift in (0, 1):
        where = [jax.random.randint(jax.random.fold_in(rng, axis), (), 0, length) for axis, length in enumerate(values.shape)]
        where[longest] = (where[longest] + shift) % values.shape[longest]
        spots.append(tuple(where))
    return values.at[spots[0]].set(low).at[spots[1]].set(high)


def shard_levels(stream_key, extent, pieces, low, top_value):
    loudness = 1.0
    for dim, parts in pieces:
        heights = jax.random.uniform(jax.random.fold_in(jax.random.fold_in(stream_key, 6), dim), (parts,), jnp.float32, low / len(pieces), top_value / len(pieces))
        loudness = loudness * jnp.repeat(jnp.exp(heights), extent[dim] // parts).reshape((-1,) + (1,) * (len(extent) - 1 - dim))
    return loudness


def noise(own_key, dims, scale, reach, cuts=(), held_as=jnp.bfloat16):
    loudness = shard_levels(own_key, dims, cuts, -0.22, 0.18) if cuts else 1.0
    entries = jax.random.normal(own_key, dims, jnp.float32) * scale * loudness
    return jnp.minimum(jnp.maximum(entries, -reach), reach).astype(held_as)


def setup_inputs(seed: int = 0) -> dict:
    keys = jax.random.split(jax.random.key(seed), 12)
    item_table = noise(keys[0], (TROWS, E), 1.0, 6.0, ((0, 128),))
    send_rows = draw_send_rows(jax.random.fold_in(keys[11], 71), 0)
    send_count = draw_send_count(jax.random.fold_in(keys[11], 71), 0)
    pos_slot = draw_pos_slot(jax.random.fold_in(keys[11], 71), 0)
    neg_slot = draw_neg_slot(jax.random.fold_in(keys[11], 71), 0)
    user_ids = plant(jax.random.randint(keys[5], (BATCH, FEAT), 0, UVOCAB), jax.random.fold_in(keys[5], 1), 0, UVOCAB - 1).astype(jnp.int32)
    user_table = noise(keys[6], (UVOCAB, E), 0.35, 2.09375)
    item_w1 = noise(keys[7], (E, H), E ** -0.5, 0.375)
    item_w2 = noise(keys[8], (H, OUTW), H ** -0.5, 0.25)
    user_w1 = noise(keys[9], (E, H), E ** -0.5, 0.375)
    user_w2 = noise(keys[10], (H, OUTW), H ** -0.5, 0.25)
    return dict(item_table=item_table, send_rows=send_rows, send_count=send_count, pos_slot=pos_slot, neg_slot=neg_slot, user_ids=user_ids, user_table=user_table, item_w1=item_w1, item_w2=item_w2, user_w1=user_w1, user_w2=user_w2)


LOGIT_SCALE = 20.0
NORM_EPS = 1e-06

def tower(inputs, first_w, second_w):
    preact = jnp.dot(inputs, first_w, preferred_element_type=jnp.float32)
    hidden = jax.nn.silu(preact).astype(jnp.bfloat16)
    output = jnp.dot(hidden, second_w, preferred_element_type=jnp.float32)
    length = jnp.sqrt(lax.optimization_barrier(jnp.sum(output * output, axis=-1, keepdims=True)) + NORM_EPS)
    return (preact, length, output / length)

def arrivals(item_table, send_rows, send_count, target):
    owners = jnp.arange(PEERS, dtype=jnp.int32)[:, None]
    flat_ids = owners * ROWS_DEV + send_rows[:, target, :]
    fetched = item_table[flat_ids]
    live_mask = jnp.arange(CAP, dtype=jnp.int32)[None, :] < send_count[:, target][:, None]
    return (fetched * live_mask[..., None].astype(jnp.bfloat16)).reshape(PEERS * CAP, E)

def reference(item_table, send_rows, send_count, pos_slot, neg_slot, user_ids, user_table, item_w1, item_w2, user_w1, user_w2):
    targets = jnp.arange(PEERS, dtype=jnp.int32)
    pos_all = pos_slot.reshape(PEERS, B_DEV)
    ids_all = user_ids.reshape(PEERS, B_DEV, FEAT)

    def forward_one(target):
        item_rows = arrivals(item_table, send_rows, send_count, target)
        item_vec = tower(item_rows, item_w1, item_w2)[2].astype(jnp.bfloat16)
        positive = item_vec[pos_all[target]]
        negative = item_vec[neg_slot[target]]
        pooled = lax.optimization_barrier(jnp.sum(user_table[ids_all[target]].astype(jnp.float32), axis=1)).astype(jnp.bfloat16)
        queries = tower(pooled, user_w1, user_w2)[2].astype(jnp.bfloat16)
        return (positive, negative, queries)
    positives, negatives, all_queries = lax.map(forward_one, targets)
    grouped = positives.reshape(N_GRP, N_REP, B_DEV, OUTW)
    col_total = N_GRP * B_DEV + NEG

    def logits_one(target):
        grp_index = target // N_REP
        rep_index = target % N_REP
        in_batch = lax.dynamic_index_in_dim(grouped, rep_index, 1, keepdims=False).reshape(N_GRP * B_DEV, OUTW)
        columns = jnp.concatenate([in_batch, negatives[target]], axis=0)
        queries = all_queries[target]
        scores = LOGIT_SCALE * jnp.dot(queries, columns.T, preferred_element_type=jnp.float32)
        log_total = jnp.log(lax.optimization_barrier(jnp.sum(jnp.exp(scores), axis=1)))
        label_cols = (grp_index * B_DEV + jnp.arange(B_DEV, dtype=jnp.int32)).astype(jnp.int32)
        picked = jnp.take_along_axis(scores, label_cols[:, None], axis=1)[:, 0]
        onehot = (jnp.arange(col_total, dtype=jnp.int32)[None, :] == label_cols[:, None]).astype(jnp.float32)
        slope = (LOGIT_SCALE * (jnp.exp(scores - log_total[:, None]) - onehot)).astype(jnp.bfloat16)
        back_cols = jnp.dot(slope.T, queries, preferred_element_type=jnp.float32)
        return (log_total - picked, back_cols[:N_GRP * B_DEV], back_cols[N_GRP * B_DEV:])
    losses, back_pos, back_neg = lax.map(logits_one, targets)
    pos_grad = lax.optimization_barrier(jnp.sum(back_pos.reshape(N_GRP, N_REP, N_GRP, B_DEV, OUTW), axis=0))
    pos_grad = jnp.transpose(pos_grad, (1, 0, 2, 3)).reshape(PEERS, B_DEV, OUTW)

    def backward_one(target):
        item_rows = arrivals(item_table, send_rows, send_count, target)
        preact, length, unit = tower(item_rows, item_w1, item_w2)
        slot_grads = jnp.zeros((PEERS * CAP, OUTW), jnp.float32)
        slot_grads = slot_grads.at[pos_all[target]].add(pos_grad[target]).at[neg_slot[target]].add(back_neg[target])
        radial = lax.optimization_barrier(jnp.sum(unit * slot_grads, axis=-1, keepdims=True))
        d_output = ((slot_grads - unit * radial) / length).astype(jnp.bfloat16)
        d_hidden = jnp.dot(d_output, item_w2.T, preferred_element_type=jnp.float32)
        sigmoid_pre = jax.nn.sigmoid(preact)
        d_pre = (d_hidden * sigmoid_pre * (1.0 + preact * (1.0 - sigmoid_pre))).astype(jnp.bfloat16)
        d_items = jnp.dot(d_pre, item_w1.T, preferred_element_type=jnp.float32).astype(jnp.bfloat16)
        return d_items.reshape(PEERS, CAP, E)
    returned = lax.map(backward_one, targets)
    by_owner = jnp.transpose(returned, (1, 0, 2, 3))
    flat_ids = (targets[:, None, None] * ROWS_DEV + send_rows).reshape(-1)
    live_mask = jnp.arange(CAP, dtype=jnp.int32)[None, None, :] < send_count[:, :, None]
    values = (by_owner.astype(jnp.float32) * live_mask[..., None].astype(jnp.float32)).reshape(-1, E)
    table_grad = jnp.zeros((TROWS, E), jnp.float32).at[flat_ids].add(values)
    return (table_grad, losses.reshape(-1))
```

```python
import jax
import jax.numpy as jnp
from jax import lax
from jax.sharding import PartitionSpec as P

LOGIT_SCALE = 20.0
NORM_EPS = 1e-06


def tower(inputs, first_w, second_w):
    preact = jnp.dot(inputs, first_w, preferred_element_type=jnp.float32)
    hidden = jax.nn.silu(preact).astype(jnp.bfloat16)
    output = jnp.dot(hidden, second_w, preferred_element_type=jnp.float32)
    length = jnp.sqrt(jnp.sum(output * output, axis=-1, keepdims=True) + NORM_EPS)
    return (preact, length, output / length)


def per_device(
    item_table,
    send_rows,
    send_count,
    pos_slot,
    neg_slot,
    user_ids,
    user_table,
    item_w1,
    item_w2,
    user_w1,
    user_w2,
):
    peer_count = lax.axis_size(("grp", "rep"))
    cap_slots = send_rows.shape[2]
    batch_rows = pos_slot.shape[0]
    row_ids = send_rows[0]
    live_mask = jnp.arange(cap_slots, dtype=jnp.int32)[None, :] < send_count[0][:, None]

    pooled = jnp.sum(user_table[user_ids].astype(jnp.float32), axis=1).astype(jnp.bfloat16)
    queries = tower(pooled, user_w1, user_w2)[2].astype(jnp.bfloat16)
    group_queries = lax.all_gather(queries, "grp", axis=0, tiled=True)

    preact, length, unit = tower(item_table, item_w1, item_w2)
    item_vec = unit.astype(jnp.bfloat16)
    outgoing = item_vec[row_ids] * live_mask[..., None].astype(jnp.bfloat16)
    arrived = lax.all_to_all(outgoing, ("grp", "rep"), split_axis=0, concat_axis=0, tiled=True)
    slot_vec = arrived.reshape(peer_count * cap_slots, -1)
    positive = slot_vec[pos_slot]
    negative = slot_vec[neg_slot[0]]

    neg_exp = jnp.exp(
        LOGIT_SCALE
        * jnp.einsum("bo,co->bc", queries, negative, preferred_element_type=jnp.float32)
    )
    user_at = jnp.arange(group_queries.shape[0], dtype=jnp.int32)[:, None]
    own_at = lax.axis_index("grp") * batch_rows + jnp.arange(batch_rows, dtype=jnp.int32)[None, :]
    pos_exp = jnp.where(
        user_at == own_at,
        0.0,
        jnp.exp(
            LOGIT_SCALE
            * jnp.einsum("bo,co->bc", group_queries, positive, preferred_element_type=jnp.float32)
        ),
    )
    other_sum = lax.psum_scatter(
        jnp.sum(pos_exp, axis=1), "grp", scatter_dimension=0, tiled=True
    ) + jnp.sum(neg_exp, axis=1)
    own_score = LOGIT_SCALE * jnp.sum(
        queries.astype(jnp.float32) * positive.astype(jnp.float32), axis=1
    )
    total = other_sum + jnp.exp(own_score)
    example_loss = jnp.log(total) - own_score
    rate = LOGIT_SCALE / total
    group_rate = lax.all_gather(rate, "grp", axis=0, tiled=True)

    neg_grad = jnp.einsum(
        "bc,bo->co",
        neg_exp.astype(jnp.bfloat16),
        (queries.astype(jnp.float32) * rate[:, None]).astype(jnp.bfloat16),
        preferred_element_type=jnp.float32,
    )
    pos_grad = jnp.einsum(
        "bc,bo->co",
        pos_exp.astype(jnp.bfloat16),
        (group_queries.astype(jnp.float32) * group_rate[:, None]).astype(jnp.bfloat16),
        preferred_element_type=jnp.float32,
    ) - (rate * other_sum)[:, None] * queries.astype(jnp.float32)

    slot_grads = jnp.zeros((peer_count * cap_slots, unit.shape[1]), jnp.float32)
    slot_grads = slot_grads.at[pos_slot].add(pos_grad).at[neg_slot[0]].add(neg_grad)
    returned = lax.all_to_all(
        slot_grads.astype(jnp.bfloat16).reshape(peer_count, cap_slots, -1),
        ("grp", "rep"),
        split_axis=0,
        concat_axis=0,
        tiled=True,
    )
    values = returned.astype(jnp.float32) * live_mask[..., None].astype(jnp.float32)
    row_grads = jnp.zeros(unit.shape, jnp.float32)
    row_grads = row_grads.at[row_ids.reshape(-1)].add(values.reshape(-1, unit.shape[1]))

    radial = jnp.sum(unit * row_grads, axis=-1, keepdims=True)
    d_output = ((row_grads - unit * radial) / length).astype(jnp.bfloat16)
    d_hidden = jnp.einsum("so,ho->sh", d_output, item_w2, preferred_element_type=jnp.float32)
    sigmoid_pre = jax.nn.sigmoid(preact)
    d_pre = (d_hidden * sigmoid_pre * (1.0 + preact * (1.0 - sigmoid_pre))).astype(jnp.bfloat16)
    table_grad = jnp.einsum("sh,eh->se", d_pre, item_w1, preferred_element_type=jnp.float32)
    return (table_grad, example_loss)


def solution(mesh):
    return jax.shard_map(
        per_device,
        mesh=mesh,
        in_specs=(
            P(("grp", "rep"), None),
            P(("grp", "rep"), None, None),
            P(("grp", "rep"), None),
            P(("grp", "rep")),
            P(("grp", "rep"), None),
            P(("grp", "rep"), None),
            P(),
            P(),
            P(),
            P(),
            P(),
        ),
        out_specs=(P(("grp", "rep"), None), P(("grp", "rep"))),
        check_vma=False,
    )
```

```python
import functools
import math

import jax
import jax.numpy as jnp
from jax import lax
from jax.experimental import pallas as pl
from jax.experimental.pallas import tpu as pltpu
from jax.sharding import PartitionSpec as P

LOGIT_SCALE = 20.0
NORM_EPS = 1e-06
LOG2E = math.log2(math.e)
MESH = pl.DeviceIdType.MESH
VMEM = pl.BlockSpec(memory_space=pltpu.VMEM)
SMEM = pl.BlockSpec(memory_space=pltpu.SMEM)
F32, BF16 = jnp.float32, jnp.bfloat16


def mm(a, b):
    return jnp.dot(a, b, preferred_element_type=F32)


def mm_t(a, b):
    return lax.dot_general(a, b, (((1,), (1,)), ((), ())), preferred_element_type=F32)


def tower(x, w1, w2):
    pre = mm(x, w1)
    sig = 0.5 + 0.5 * jnp.tanh(0.5 * pre)
    out = mm((pre * sig).astype(BF16), w2)
    inv = lax.rsqrt(jnp.sum(out * out, axis=-1, keepdims=True) + NORM_EPS)
    return pre, sig, inv, out * inv


def params(**kw):
    return pltpu.CompilerParams(vmem_limit_bytes=56 * 2**20, **kw)


def item_kernel(rows, table, w1, w2, out, unit, picked):
    n = table.shape[0]
    unit[pl.ds(n, 8), :] = jnp.zeros((8, unit.shape[1]), F32)

    def forward(i, c):
        at = pl.ds(i * 256, 256)
        unit[at, :] = tower(table[at, :], w1[...], w2[...])[3]
        return c

    lax.fori_loop(0, n // 256, forward, 0)

    def gather(t, c):
        for j in range(32):
            picked[pl.ds(t * 32 + j, 1), :] = unit[pl.ds(rows[t * 32 + j], 1), :]
        at = pl.ds(t * 32, 32)
        out[at, :] = picked[at, :].astype(BF16)
        return c

    lax.fori_loop(0, out.shape[0] // 32, gather, 0)


def user_kernel(ids, table, w1, w2, out, low, high, plow, phigh):
    half = table.shape[1] // 2
    feat = ids.shape[0] // out.shape[0]

    def widen(i, c):
        at = pl.ds(i * 128, 128)
        low[at, :] = table[at, :half].astype(F32)
        high[at, :] = table[at, half:].astype(F32)
        return c

    lax.fori_loop(0, table.shape[0] // 128, widen, 0)

    def pool(i, c):
        for k in range(8):
            b = i * 8 + k
            at = [pl.ds(ids[b * feat + f], 1) for f in range(feat)]
            lo = [low[a, :] for a in at]
            hi = [high[a, :] for a in at]
            while len(lo) > 1:
                lo = [x + y for x, y in zip(lo[::2], lo[1::2])]
                hi = [x + y for x, y in zip(hi[::2], hi[1::2])]
            plow[pl.ds(b, 1), :] = lo[0]
            phigh[pl.ds(b, 1), :] = hi[0]
        return c

    lax.fori_loop(0, out.shape[0] // 8, pool, 0)

    def forward(i, c):
        at = pl.ds(i * 256, 256)
        x = jnp.concatenate([plow[at, :], phigh[at, :]], axis=1).astype(BF16)
        out[at, :] = tower(x, w1[...], w2[...])[3].astype(BF16)
        return c

    lax.fori_loop(0, out.shape[0] // 256, forward, 0)


def score_kernel(
    pos_slot, neg_slot, queries, slots, pos_grad, neg_grad, loss,
    wide, picked, cols, group, pexp, nexp, sums_out, sums_in, rates,
    q_send, q_recv, f_send, f_recv, s_send, s_recv, r_send, r_recv,
):
    users = queries.shape[0]
    peers = group.shape[0]
    chips = peers // 2
    me = lax.axis_index("grp")
    chip, core = me // 2, lax.rem(me, 2)
    sib = chip * 2 + 1 - core

    def there(k):
        return lax.rem(chip + k, chips) * 2 + core

    barrier = pltpu.get_barrier_semaphore()
    for k in range(1, peers):
        pl.semaphore_signal(
            barrier, inc=1, device_id={"grp": lax.rem(me + k, peers)}, device_id_type=MESH
        )
    pl.semaphore_wait(barrier, peers - 1)

    def push(src, dst, ss, rs, to):
        return pltpu.make_async_remote_copy(
            src_ref=src, dst_ref=dst, send_sem=ss, recv_sem=rs,
            device_id={"grp": to}, device_id_type=MESH,
        )

    group[0] = queries[...]
    q_copies = []
    for k in range(1, chips):
        q_copies.append(
            push(queries, group.at[k], q_send.at[k], q_recv.at[k], there(chips - k))
        )
        q_copies[-1].start()
    f_copies = [push(queries, group.at[chips], f_send.at[0], f_recv.at[0], sib)]
    f_copies[0].start()
    for k in range(1, chips):
        f_copies.append(
            push(group.at[k], group.at[chips + k], f_send.at[k], f_recv.at[k], sib)
        )

    def widen(i, c):
        at = pl.ds(i * 256, 256)
        wide[at, :] = slots[at, :].astype(F32)
        return c

    lax.fori_loop(0, slots.shape[0] // 256, widen, 0)

    def gather(i, c):
        for j in range(16):
            picked[pl.ds(i * 16 + j, 1), :] = wide[pl.ds(neg_slot[i * 16 + j], 1), :]
        for j in range(16):
            picked[pl.ds(users + i * 16 + j, 1), :] = wide[pl.ds(pos_slot[i * 16 + j], 1), :]
        return c

    lax.fori_loop(0, users // 16, gather, 0)

    def narrow(i, c):
        at = pl.ds(i * 256, 256)
        cols[at, :] = picked[at, :].astype(BF16)
        return c

    lax.fori_loop(0, cols.shape[0] // 256, narrow, 0)

    step = 128

    def block(q, first, store, diag):
        def part(i, carry):
            total, own = carry
            s = mm_t(cols[pl.ds(first + i * step, step), :], q)
            e = jnp.exp2(s * (LOGIT_SCALE * LOG2E))
            if diag:
                hit = (
                    lax.broadcasted_iota(jnp.int32, s.shape, 0) + i * step
                    == lax.broadcasted_iota(jnp.int32, s.shape, 1)
                )
                e = jnp.where(hit, 0.0, e)
                own = own + jnp.sum(jnp.where(hit, s, 0.0), axis=0, keepdims=True)
            store(i, e.astype(BF16))
            return total + jnp.sum(e, axis=0, keepdims=True), own

        zero = jnp.zeros((1, users), F32)
        return lax.fori_loop(0, users // step, part, (zero, zero))

    def store_neg(i, e):
        nexp[pl.ds(i * step, step), :] = e

    def store_pos(k):
        def store(i, e):
            pexp[k, pl.ds(i * step, step), :] = e

        return store

    neg_sum, _ = block(group[0], 0, store_neg, False)
    own_sum, own_score = block(group[0], users, store_pos(0), True)
    own_score = own_score * LOGIT_SCALE

    s_copies = []
    order = [chips]
    for k in range(1, chips):
        order += [k, chips + k]
    for k in order:
        if k >= chips:
            f_copies[k - chips].wait_recv()
        else:
            q_copies[k - 1].wait_recv()
            f_copies[k].start()
        total, _ = block(group[k], users, store_pos(k), False)
        sums_out[k] = total
        kk = k % chips
        back = (chips - kk) % chips + (chips if k >= chips else 0)
        to = lax.rem(chip + kk, chips) * 2 + (1 - core if k >= chips else core)
        s_copies.append(push(sums_out.at[k], sums_in.at[back], s_send.at[k], s_recv.at[back], to))
        s_copies[-1].start()
    for c in s_copies:
        c.wait_recv()

    other = neg_sum + own_sum
    for k in range(1, peers):
        other = other + sums_in[k]
    total = other + jnp.exp2(own_score * LOG2E)
    loss[...] = jnp.log(total) - own_score
    rate = LOGIT_SCALE / total
    rates[0] = rate
    r_copies = []
    for k in order:
        kk = k % chips
        back = (chips - kk) % chips + (chips if k >= chips else 0)
        to = lax.rem(chip + kk, chips) * 2 + (1 - core if k >= chips else core)
        r_copies.append(push(rates.at[0], rates.at[back], r_send.at[k], r_recv.at[back], to))
        r_copies[-1].start()

    def upright(row):
        return jnp.transpose(jnp.broadcast_to(row, (128, users)))

    q_own = group[0].astype(F32)
    scaled = (q_own * upright(rate)).astype(BF16)

    def own_part(i, c):
        at = pl.ds(i * 256, 256)
        neg_grad[at, :] = mm(nexp[at, :], scaled)
        pos_grad[at, :] = mm(pexp[0, at, :], scaled)
        return c

    lax.fori_loop(0, users // 256, own_part, 0)
    pos_grad[...] = pos_grad[...] - q_own * upright(rate * other)

    for c in r_copies:
        c.wait_recv()

    for k in order:
        scaled_k = (group[k].astype(F32) * upright(rates[k])).astype(BF16)

        def far_part(i, c):
            at = pl.ds(i * 256, 256)
            pos_grad[at, :] = pos_grad[at, :] + mm(pexp[k, at, :], scaled_k)
            return c

        lax.fori_loop(0, users // 256, far_part, 0)

    for c in q_copies + f_copies + s_copies + r_copies:
        c.wait_send()


def slot_kernel(pos_slot, neg_slot, pos_grad, neg_grad, out, *acc):
    n = out.shape[0]
    half = pos_slot.shape[0] // 2

    def clear(i, c):
        for a in acc:
            a[pl.ds(i * 128, 128), :] = jnp.zeros((128, a.shape[1]), F32)
        return c

    lax.fori_loop(0, n // 128, clear, 0)
    chains = [
        (pos_slot, pos_grad, 0), (neg_slot, neg_grad, 0),
        (pos_slot, pos_grad, half), (neg_slot, neg_grad, half),
    ]

    def scatter(i, c):
        for j in range(8):
            at = [pl.ds(slot[first + i * 8 + j], 1) for slot, _, first in chains]
            new = [
                a[r, :] + grad[pl.ds(first + i * 8 + j, 1), :]
                for a, r, (_, grad, first) in zip(acc, at, chains)
            ]
            for a, r, v in zip(acc, at, new):
                a[r, :] = v
        return c

    lax.fori_loop(0, half // 8, scatter, 0)

    def merge(i, c):
        at = pl.ds(i * 128, 128)
        out[at, :] = (acc[0][at, :] + acc[1][at, :] + (acc[2][at, :] + acc[3][at, :])).astype(BF16)
        return c

    lax.fori_loop(0, n // 128, merge, 0)


def back_kernel(rows, back, table, w1, w2, out, acc, wide):
    n = table.shape[0]

    def prepare(i, c):
        at = pl.ds(i * 128, 128)
        acc[at, :] = jnp.zeros((128, acc.shape[1]), F32)
        wide[at, :] = back[at, :].astype(F32)
        return c

    lax.fori_loop(0, n // 128, prepare, 0)

    def scatter(t, c):
        at = [pl.ds(rows[t * 32 + j], 1) for j in range(32)]
        new = [acc[r, :] + wide[pl.ds(t * 32 + j, 1), :] for j, r in enumerate(at)]
        for r, v in zip(at, new):
            acc[r, :] = v
        return c

    lax.fori_loop(0, wide.shape[0] // 32, scatter, 0)

    def backward(i, c):
        at = pl.ds(i * 256, 256)
        pre, sig, inv, unit = tower(table[at, :], w1[...], w2[...])
        g = acc[at, :]
        radial = jnp.sum(unit * g, axis=-1, keepdims=True)
        d_out = ((g - unit * radial) * inv).astype(BF16)
        d_hid = mm_t(d_out, w2[...])
        d_pre = (d_hid * sig * (1.0 + pre * (1.0 - sig))).astype(BF16)
        out[at, :] = mm_t(d_pre, w1[...])
        return c

    lax.fori_loop(0, n // 256, backward, 0)


def per_device(
    item_table, send_rows, send_count, pos_slot, neg_slot, user_ids,
    user_table, item_w1, item_w2, user_w1, user_w2,
):
    peers, cap = send_rows.shape[1:]
    slots = peers * cap
    n, users, negs = item_table.shape[0], pos_slot.shape[0], neg_slot.shape[1]
    vocab, outw = user_table.shape[0], item_w2.shape[1]
    grp = lax.axis_size("grp")
    live = jnp.arange(cap, dtype=jnp.int32)[None, :] < send_count[0][:, None]
    rows = jnp.where(live, send_rows[0], n).reshape(-1)
    neg = neg_slot.reshape(-1)

    outgoing = pl.pallas_call(
        item_kernel,
        out_shape=jax.ShapeDtypeStruct((slots, outw), BF16),
        in_specs=[SMEM] + [VMEM] * 3,
        out_specs=VMEM,
        scratch_shapes=[pltpu.VMEM((n + 8, outw), F32), pltpu.VMEM((slots, outw), F32)],
        compiler_params=params(),
        cost_estimate=pl.CostEstimate(flops=2 * n * 512 * 384, bytes_accessed=2**22, transcendentals=n * 512),
        name="items",
    )(rows, item_table, item_w1, item_w2)
    arrived = lax.all_to_all(
        outgoing.reshape(peers, cap, outw), ("grp", "rep"), split_axis=0, concat_axis=0, tiled=True
    ).reshape(slots, outw)

    queries = pl.pallas_call(
        user_kernel,
        out_shape=jax.ShapeDtypeStruct((users, outw), BF16),
        in_specs=[SMEM] + [VMEM] * 3,
        out_specs=VMEM,
        scratch_shapes=[pltpu.VMEM((vocab, 128), F32)] * 2 + [pltpu.VMEM((users, 128), F32)] * 2,
        compiler_params=params(),
        cost_estimate=pl.CostEstimate(flops=2**33, bytes_accessed=2**24, transcendentals=users * 512),
        name="users",
    )(user_ids.reshape(-1), user_table, user_w1, user_w2)

    dma = pltpu.SemaphoreType.DMA
    pos_grad, neg_grad, loss = pl.pallas_call(
        score_kernel,
        out_shape=[
            jax.ShapeDtypeStruct((users, outw), F32),
            jax.ShapeDtypeStruct((negs, outw), F32),
            jax.ShapeDtypeStruct((1, users), F32),
        ],
        in_specs=[SMEM, SMEM, VMEM, VMEM],
        out_specs=[VMEM] * 3,
        scratch_shapes=[
            pltpu.VMEM((slots, outw), F32),
            pltpu.VMEM((users + negs, outw), F32),
            pltpu.VMEM((users + negs, outw), BF16),
            pltpu.VMEM((grp, users, outw), BF16),
            pltpu.VMEM((grp, users, users), BF16),
            pltpu.VMEM((negs, users), BF16),
            pltpu.VMEM((grp, 1, users), F32),
            pltpu.VMEM((grp, 1, users), F32),
            pltpu.VMEM((grp, 1, users), F32),
            dma((grp // 2,)), dma((grp // 2,)), dma((grp // 2,)), dma((grp // 2,)),
            dma((grp,)), dma((grp,)), dma((grp,)), dma((grp,)),
        ],
        compiler_params=params(collective_id=0, has_side_effects=True),
        cost_estimate=pl.CostEstimate(flops=2**32, bytes_accessed=2**22, transcendentals=2**23),
        name="scores",
    )(pos_slot, neg, queries, arrived)

    slot_grads = pl.pallas_call(
        slot_kernel,
        out_shape=jax.ShapeDtypeStruct((slots, outw), BF16),
        in_specs=[SMEM, SMEM, VMEM, VMEM],
        out_specs=VMEM,
        scratch_shapes=[pltpu.VMEM((slots, outw), F32)] * 4,
        compiler_params=params(),
        name="slot_sums",
    )(pos_slot, neg, pos_grad, neg_grad)
    returned = lax.all_to_all(
        slot_grads.reshape(peers, cap, outw), ("grp", "rep"), split_axis=0, concat_axis=0, tiled=True
    ).reshape(slots, outw)

    table_grad = pl.pallas_call(
        back_kernel,
        out_shape=jax.ShapeDtypeStruct(item_table.shape, F32),
        in_specs=[SMEM] + [VMEM] * 4,
        out_specs=VMEM,
        scratch_shapes=[pltpu.VMEM((n + 8, outw), F32), pltpu.VMEM((slots, outw), F32)],
        compiler_params=params(),
        name="row_grads",
    )(rows, returned, item_table, item_w1, item_w2)
    return table_grad, loss.reshape(-1)


def solution(mesh):
    return jax.shard_map(
        per_device,
        mesh=mesh,
        in_specs=(
            P(("grp", "rep"), None),
            P(("grp", "rep"), None, None),
            P(("grp", "rep"), None),
            P(("grp", "rep")),
            P(("grp", "rep"), None),
            P(("grp", "rep"), None),
            P(), P(), P(), P(), P(),
        ),
        out_specs=(P(("grp", "rep"), None), P(("grp", "rep"))),
        check_vma=False,
    )
```

```python
import math

import jax
import jax.numpy as jnp
from jax import lax
from jax.experimental import pallas as pl
from jax.experimental.pallas import tpu as pltpu
from jax.sharding import PartitionSpec as P

LOGIT_SCALE = 20.0
NORM_EPS = 1e-06
LOG2E = math.log2(math.e)
MESH = pl.DeviceIdType.MESH
VMEM = pl.BlockSpec(memory_space=pltpu.VMEM)
SMEM = pl.BlockSpec(memory_space=pltpu.SMEM)
ANY = pl.BlockSpec(memory_space=pl.ANY)
F32, BF16 = jnp.float32, jnp.bfloat16
TILE = 1024
GROUPS = 8


def mm(a, b):
    return jnp.dot(a, b, preferred_element_type=F32)


def mm_t(a, b):
    return lax.dot_general(a, b, (((1,), (1,)), ((), ())), preferred_element_type=F32)


def tower(x, w1, w2):
    pre = mm(x, w1)
    sig = 0.5 + 0.5 * jnp.tanh(0.5 * pre)
    out = mm((pre * sig).astype(BF16), w2)
    inv = lax.rsqrt(jnp.sum(out * out, axis=-1, keepdims=True) + NORM_EPS)
    return pre, sig, inv, out * inv


def upright(row):
    return jnp.transpose(jnp.broadcast_to(row, (128, row.shape[1])))


def spread(at, grads):
    half = 2048
    low = jnp.where(at >= half, at - half, at)
    hot = jnp.where(
        lax.broadcasted_iota(jnp.int32, (half, at.shape[1]), 0) == low, 1.0, 0.0
    ).astype(BF16)
    upper = upright(at.astype(F32)) >= half
    grads = grads.astype(F32)
    both = jnp.concatenate(
        [jnp.where(upper, 0.0, grads), jnp.where(upper, grads, 0.0)], axis=1
    ).astype(BF16)
    return mm(hot, both)


def window_kernel(
    rows, pos_slot, neg_slot, ids, table, w1, w2, u1, u2, row_at, pos_at, neg_at, user_table,
    out, loss,
    ut, low, high, plow, phigh, unit, wide, send, recv, cols, group, pexp, nexp, scaled,
    sums_out, sums_in, rates, acc, back_send, back_recv,
    t_sem, o_sem, a_send, a_recv, b_send, b_recv, l_sem,
    q_send, q_recv, f_send, f_recv, s_send, s_recv, r_send, r_recv,
):
    n, users = table.shape[0], group.shape[1]
    cap = 32
    grp, rep = lax.axis_size("grp"), lax.axis_size("rep")
    peers = grp * rep
    chips = grp // 2
    g, r = lax.axis_index("grp"), lax.axis_index("rep")
    me = g * rep + r
    chip, core = g // 2, lax.rem(g, 2)

    def place(t):
        return (t // rep, lax.rem(t, rep))

    barrier = pltpu.get_barrier_semaphore()

    def greet(k, c):
        pl.semaphore_signal(
            barrier, inc=1, device_id=place(lax.rem(me + k, peers)), device_id_type=MESH
        )
        return c

    lax.fori_loop(1, peers, greet, 0)
    fetch = pltpu.make_async_copy(user_table, ut, t_sem)
    fetch.start()

    unit[pl.ds(n, 8), :] = jnp.zeros((8, unit.shape[1]), F32)

    def forward(i, c):
        at = pl.ds(pl.multiple_of(i * TILE, TILE), TILE)
        unit[at, :] = tower(table[at, :], w1[...], w2[...])[3]
        return c

    lax.fori_loop(0, n // TILE, forward, 0)
    pl.semaphore_wait(barrier, peers - 1)

    def span(t):
        return pl.ds(pl.multiple_of(t * cap, cap), cap)

    def gather_list(t):
        for j in range(cap):
            wide[pl.ds(t * cap + j, 1), :] = unit[pl.ds(rows[t * cap + j], 1), :]
        send[span(t), :] = wide[span(t), :].astype(BF16)

    def send_list(k, c):
        t = lax.rem(me + k, peers)
        gather_list(t)
        pltpu.make_async_remote_copy(
            src_ref=send.at[span(t), :], dst_ref=recv.at[span(me), :],
            send_sem=a_send, recv_sem=a_recv, device_id=place(t), device_id_type=MESH,
        ).start()
        return c

    lax.fori_loop(1, peers, send_list, 0)
    gather_list(me)
    keep = pltpu.make_async_copy(send.at[span(me), :], recv.at[span(me), :], l_sem)
    keep.start()

    fetch.wait()

    def widen(i, c):
        at = pl.ds(pl.multiple_of(i * 256, 256), 256)
        low[at, :] = ut[at, :128].astype(F32)
        high[at, :] = ut[at, 128:].astype(F32)
        return c

    lax.fori_loop(0, ut.shape[0] // 256, widen, 0)

    def pool(i, c):
        for k in range(8):
            b = i * 8 + k
            at = [pl.ds(ids[f, b], 1) for f in range(ids.shape[0])]
            lo = [low[a, :] for a in at]
            hi = [high[a, :] for a in at]
            while len(lo) > 1:
                lo = [x + y for x, y in zip(lo[::2], lo[1::2])]
                hi = [x + y for x, y in zip(hi[::2], hi[1::2])]
            plow[pl.ds(b, 1), :] = lo[0]
            phigh[pl.ds(b, 1), :] = hi[0]
        return c

    lax.fori_loop(0, users // 8, pool, 0)
    pooled = jnp.concatenate([plow[...], phigh[...]], axis=1).astype(BF16)
    group[0] = tower(pooled, u1[...], u2[...])[3].astype(BF16)

    far = sorted(range(1, chips), key=lambda k: (min(k, chips - k), k))
    names = [(0, 0), (0, 1)] + [(k, 0) for k in far] + [(k, 1) for k in far]
    slot_of = {name: i for i, name in enumerate(names)}

    def push(src, dst, ss, rs, k, flip):
        to = lax.rem(chip + k, chips) * 2 + (1 - core if flip else core)
        return pltpu.make_async_remote_copy(
            src_ref=src, dst_ref=dst, send_sem=ss, recv_sem=rs,
            device_id=(to, r), device_id_type=MESH,
        )

    f_copies = {0: push(group.at[0], group.at[1], f_send.at[0], f_recv.at[0], 0, 1)}
    q_copies = {}
    for k in far:
        s = slot_of[(k, 0)]
        q_copies[k] = push(group.at[0], group.at[s], q_send.at[k], q_recv.at[k], chips - k, 0)
        f_copies[k] = push(group.at[s], group.at[slot_of[(k, 1)]], f_send.at[k], f_recv.at[k], 0, 1)
        q_copies[k].start()
    f_copies[0].start()

    keep.wait()
    others = pl.ds(0, (peers - 1) * cap)
    pltpu.make_async_copy(send.at[others, :], recv.at[others, :], a_recv).wait()
    wide[...] = recv[...].astype(F32)

    def pick(i, c):
        for j in range(32):
            low[pl.ds(i * 32 + j, 1), :] = wide[pl.ds(neg_slot[i * 32 + j], 1), :]
        for j in range(32):
            low[pl.ds(users + i * 32 + j, 1), :] = wide[pl.ds(pos_slot[i * 32 + j], 1), :]
        return c

    lax.fori_loop(0, users // 32, pick, 0)
    cols[...] = low[pl.ds(0, 2 * users), :].astype(BF16)

    s = mm_t(cols[pl.ds(0, users), :], group[0])
    e = jnp.exp2(s * (LOGIT_SCALE * LOG2E))
    nexp[...] = e.astype(BF16)
    other = jnp.sum(e, axis=0, keepdims=True)
    s = mm_t(cols[pl.ds(users, users), :], group[0])
    hit = lax.broadcasted_iota(jnp.int32, s.shape, 0) == lax.broadcasted_iota(jnp.int32, s.shape, 1)
    e = jnp.where(hit, 0.0, jnp.exp2(s * (LOGIT_SCALE * LOG2E)))
    own_score = jnp.sum(jnp.where(hit, s, 0.0), axis=0, keepdims=True) * LOGIT_SCALE
    pexp[0] = e.astype(BF16)
    other = other + jnp.sum(e, axis=0, keepdims=True)

    s_copies = []

    def compute(first, last):
        def one(k, c):
            s = mm_t(cols[pl.ds(users, users), :], group[k])
            e = jnp.exp2(s * (LOGIT_SCALE * LOG2E))
            pexp[k] = e.astype(BF16)
            sums_out[k] = jnp.sum(e, axis=0, keepdims=True)
            return c

        lax.fori_loop(first, last, one, 0)
        for i in range(first, last):
            k, flip = names[i]
            b = slot_of[((chips - k) % chips, flip)]
            s_copies.append(push(sums_out.at[i], sums_in.at[b], s_send.at[i], s_recv.at[b], k, flip))
            s_copies[-1].start()

    f_copies[0].wait_recv()
    compute(1, 2)
    for k in far:
        q_copies[k].wait_recv()
        f_copies[k].start()
    compute(2, 1 + chips)
    for k in far:
        f_copies[k].wait_recv()
    compute(1 + chips, grp)
    for c in s_copies:
        c.wait_recv()

    for k in range(1, grp):
        other = other + sums_in[k]
    total = other + jnp.exp2(own_score * LOG2E)
    loss[...] = jnp.log(total) - own_score
    rate = LOGIT_SCALE / total
    rates[0] = rate
    r_copies = []
    for i in range(1, grp):
        k, flip = names[i]
        b = slot_of[((chips - k) % chips, flip)]
        r_copies.append(push(rates.at[0], rates.at[b], r_send.at[i], r_recv.at[b], k, flip))
        r_copies[-1].start()

    scaled[0] = (group[0].astype(F32) * upright(rate)).astype(BF16)
    acc[...] = spread(neg_at[...], mm(nexp[...], scaled[0]))
    own = group[0].astype(F32) * upright(rate * other)
    for c in r_copies:
        c.wait_recv()

    def scale(k, c):
        scaled[k] = (group[k].astype(F32) * upright(rates[k])).astype(BF16)
        return c

    lax.fori_loop(1, grp, scale, 0)
    grads = mm(pexp[0], scaled[0]) - own
    for k in range(1, grp):
        grads = grads + mm(pexp[k], scaled[k])
    total_grads = acc[...] + spread(pos_at[...], grads)
    half = n // 2
    back_send[pl.ds(0, half), :] = total_grads[:, :128].astype(BF16)
    back_send[pl.ds(half, half), :] = total_grads[:, 128:].astype(BF16)

    per = peers // GROUPS

    def send_back(k, c):
        t = lax.rem(me + k, peers)
        pltpu.make_async_remote_copy(
            src_ref=back_send.at[span(t), :], dst_ref=back_recv.at[span(me), :],
            send_sem=b_send, recv_sem=b_recv.at[me // per], device_id=place(t), device_id_type=MESH,
        ).start()
        return c

    lax.fori_loop(1, peers, send_back, 0)
    keep = pltpu.make_async_copy(
        back_send.at[span(me), :], back_recv.at[span(me), :], b_recv.at[me // per]
    )
    keep.start()

    def slope(i, c):
        at = pl.ds(pl.multiple_of(i * TILE, TILE), TILE)
        pre, sig, inv, _ = tower(table[at, :], w1[...], w2[...])
        pexp[i, :, :512] = (sig * (1.0 + pre * (1.0 - sig)) * inv).astype(BF16)
        return c

    lax.fori_loop(0, n // TILE, slope, 0)

    acc[...] = jnp.zeros(acc.shape, F32)

    def arrive(i, c):
        b = lax.rem(me // per + 2 * GROUPS - 1 - i, GROUPS)
        at = pl.ds(pl.multiple_of(b * (per * cap), per * cap), per * cap)
        pltpu.make_async_copy(back_send.at[at, :], back_recv.at[at, :], b_recv.at[b]).wait()
        acc[...] = acc[...] + spread(row_at[pl.ds(b, 1), :], back_recv[at, :])
        return c

    lax.fori_loop(0, GROUPS, arrive, 0)

    o_copies = []
    for i in range(n // TILE):
        at = pl.ds(i * TILE, TILE)
        side = i * TILE // half * 128
        grad = acc[pl.ds(i * TILE % half, TILE), side:side + 128]
        u = unit[at, :]
        d_out = (grad - u * jnp.sum(u * grad, axis=-1, keepdims=True)).astype(BF16)
        d_pre = (mm_t(d_out, w2[...]) * pexp[i, :, :512].astype(F32)).astype(BF16)
        d_row = mm_t(d_pre, w1[...])
        low[at, :] = d_row[:, :128]
        high[at, :] = d_row[:, 128:]
        o_copies += [
            pltpu.make_async_copy(low.at[at, :], out.at[at, pl.ds(0, 128)], o_sem.at[2 * i]),
            pltpu.make_async_copy(high.at[at, :], out.at[at, pl.ds(128, 128)], o_sem.at[2 * i + 1]),
        ]
        o_copies[-2].start()
        o_copies[-1].start()

    for c in list(q_copies.values()) + list(f_copies.values()) + s_copies + r_copies:
        c.wait_send()
    pltpu.make_async_copy(send.at[others, :], recv.at[others, :], a_send).wait()
    pltpu.make_async_copy(back_send.at[others, :], back_recv.at[others, :], b_send).wait()
    for c in o_copies:
        c.wait()


def per_device(
    item_table, send_rows, send_count, pos_slot, neg_slot, user_ids,
    user_table, item_w1, item_w2, user_w1, user_w2,
):
    peers, cap = send_rows.shape[1:]
    slots = peers * cap
    n, users = item_table.shape[0], pos_slot.shape[0]
    vocab, outw = user_table.shape[0], item_w2.shape[1]
    grp = lax.axis_size("grp")
    chips = grp // 2
    live = jnp.arange(cap, dtype=jnp.int32)[:, None] < send_count
    rows = jnp.where(live, send_rows[0].T, n).T.reshape(-1)
    neg = neg_slot.reshape(-1)

    dma = pltpu.SemaphoreType.DMA
    vm = pltpu.VMEM
    table_grad, loss = pl.pallas_call(
        window_kernel,
        out_shape=[
            jax.ShapeDtypeStruct(item_table.shape, F32),
            jax.ShapeDtypeStruct((1, users), F32),
        ],
        in_specs=[SMEM] * 4 + [VMEM] * 8 + [ANY],
        out_specs=[ANY, VMEM],
        scratch_shapes=[
            vm(user_table.shape, BF16), vm((vocab, 128), F32), vm((vocab, 128), F32),
            vm((users, 128), F32), vm((users, 128), F32),
            vm((n + 8, outw), F32), vm((slots, outw), F32),
            vm((slots, outw), BF16), vm((slots, outw), BF16),
            vm((2 * users, outw), BF16),
            vm((grp, users, outw), BF16), vm((grp, users, users), BF16), vm((users, users), BF16),
            vm((grp, users, outw), BF16),
            vm((grp, 1, users), F32), vm((grp, 1, users), F32), vm((grp, 1, users), F32),
            vm((n // 2, 2 * outw), F32),
            vm((slots, outw), BF16), vm((slots, outw), BF16),
            dma, dma((2 * n // TILE,)), dma, dma, dma, dma((GROUPS,)), dma,
            dma((chips,)), dma((chips,)), dma((chips,)), dma((chips,)),
            dma((grp,)), dma((grp,)), dma((grp,)), dma((grp,)),
        ],
        compiler_params=pltpu.CompilerParams(
            collective_id=0, has_side_effects=True, vmem_limit_bytes=60 * 2**20
        ),
        cost_estimate=pl.CostEstimate(flops=2**34, bytes_accessed=2**24, transcendentals=2**24),
        name="window",
    )(
        rows, pos_slot, neg, user_ids.T, item_table, item_w1, item_w2, user_w1, user_w2,
        rows.reshape(GROUPS, -1), pos_slot.reshape(1, -1), neg_slot, user_table,
    )
    return table_grad, loss.reshape(-1)


def solution(mesh):
    return jax.shard_map(
        per_device,
        mesh=mesh,
        in_specs=(
            P(("grp", "rep"), None),
            P(("grp", "rep"), None, None),
            P(("grp", "rep"), None),
            P(("grp", "rep")),
            P(("grp", "rep"), None),
            P(("grp", "rep"), None),
            P(), P(), P(), P(), P(),
        ),
        out_specs=(P(("grp", "rep"), None), P(("grp", "rep"))),
        check_vma=False,
    )
```

```python
import math

import jax
import jax.numpy as jnp
from jax import lax
from jax.experimental import pallas as pl
from jax.experimental.pallas import tpu as pltpu
from jax.sharding import PartitionSpec as P

LOGIT_SCALE = 20.0
NORM_EPS = 1e-06
LOG2E = math.log2(math.e)
MESH = pl.DeviceIdType.MESH
VMEM = pl.BlockSpec(memory_space=pltpu.VMEM)
SMEM = pl.BlockSpec(memory_space=pltpu.SMEM)
ANY = pl.BlockSpec(memory_space=pl.ANY)
F32, BF16 = jnp.float32, jnp.bfloat16
TILE = 1024
GROUPS = 8


def mm(a, b):
    return jnp.dot(a, b, preferred_element_type=F32)


def mm_t(a, b):
    return lax.dot_general(a, b, (((1,), (1,)), ((), ())), preferred_element_type=F32)


def tower(x, w1, w2):
    pre = mm(x, w1)
    sig = 0.5 + 0.5 * jnp.tanh(0.5 * pre)
    out = mm((pre * sig).astype(BF16), w2)
    inv = lax.rsqrt(jnp.sum(out * out, axis=-1, keepdims=True) + NORM_EPS)
    return pre, sig, inv, out * inv


def upright(row):
    return jnp.transpose(jnp.broadcast_to(row, (128, row.shape[1])))


def spread(at, grads):
    half = 2048
    low = jnp.where(at >= half, at - half, at)
    hot = jnp.where(
        lax.broadcasted_iota(jnp.int32, (half, at.shape[1]), 0) == low, 1.0, 0.0
    ).astype(BF16)
    upper = upright(at.astype(F32)) >= half
    grads = grads.astype(F32)
    both = jnp.concatenate(
        [jnp.where(upper, 0.0, grads), jnp.where(upper, grads, 0.0)], axis=1
    ).astype(BF16)
    return mm(hot, both)


def window_kernel(
    pos_slot, neg_slot, ids, lists, counts, table, w1, w2, u1, u2, pos_at, neg_at, user_table,
    d_out, slopes, loss,
    ut, low, high, plow, phigh, unit, wide, send, recv, cols, group, pexp, nexp, scaled,
    sums_out, sums_in, rates, acc, back_send, back_recv, live_rows, rows, row_at,
    t_sem, i_sem, o_sem, a_send, a_recv, b_send, b_recv, l_sem,
    q_send, q_recv, f_send, f_recv, s_send, s_recv, r_send, r_recv,
):
    n, users = table.shape[0], group.shape[1]
    cap = 32
    grp, rep = lax.axis_size("grp"), lax.axis_size("rep")
    peers = grp * rep
    chips = grp // 2
    g, r = lax.axis_index("grp"), lax.axis_index("rep")
    me = g * rep + r
    chip, core = g // 2, lax.rem(g, 2)

    def place(t):
        return (t // rep, lax.rem(t, rep))

    barrier = pltpu.get_barrier_semaphore()

    def greet(k, c):
        pl.semaphore_signal(
            barrier, inc=1, device_id=place(lax.rem(me + k, peers)), device_id_type=MESH
        )
        return c

    lax.fori_loop(1, peers, greet, 0)
    fetch = pltpu.make_async_copy(user_table, ut, t_sem)
    fetch.start()

    live = lax.broadcasted_iota(jnp.int32, lists.shape, 0) < counts[...]
    live_rows[...] = jnp.where(live, lists[...], n)
    index = pltpu.make_async_copy(live_rows, rows, i_sem)
    index.start()

    o_copies = []
    fetch.wait()

    def widen(i, c):
        at = pl.ds(pl.multiple_of(i * 256, 256), 256)
        low[at, :] = ut[at, :128].astype(F32)
        high[at, :] = ut[at, 128:].astype(F32)
        return c

    lax.fori_loop(0, ut.shape[0] // 256, widen, 0)

    def pool(i, c):
        for k in range(8):
            b = i * 8 + k
            at = [pl.ds(ids[f, b], 1) for f in range(ids.shape[0])]
            lo = [low[a, :] for a in at]
            hi = [high[a, :] for a in at]
            while len(lo) > 1:
                lo = [x + y for x, y in zip(lo[::2], lo[1::2])]
                hi = [x + y for x, y in zip(hi[::2], hi[1::2])]
            plow[pl.ds(b, 1), :] = lo[0]
            phigh[pl.ds(b, 1), :] = hi[0]
        return c

    lax.fori_loop(0, users // 8, pool, 0)
    pooled = jnp.concatenate([plow[...], phigh[...]], axis=1).astype(BF16)
    group[0] = tower(pooled, u1[...], u2[...])[3].astype(BF16)

    far = sorted(range(1, chips), key=lambda k: (min(k, chips - k), k))
    names = [(0, 0), (0, 1)] + [(k, 0) for k in far] + [(k, 1) for k in far]
    slot_of = {name: i for i, name in enumerate(names)}

    def push(src, dst, ss, rs, k, flip):
        to = lax.rem(chip + k, chips) * 2 + (1 - core if flip else core)
        return pltpu.make_async_remote_copy(
            src_ref=src, dst_ref=dst, send_sem=ss, recv_sem=rs,
            device_id=(to, r), device_id_type=MESH,
        )

    f_copies = {0: push(group.at[0], group.at[1], f_send.at[0], f_recv.at[0], 0, 1)}
    q_copies = {}
    for k in far:
        s = slot_of[(k, 0)]
        q_copies[k] = push(group.at[0], group.at[s], q_send.at[k], q_recv.at[k], chips - k, 0)
        f_copies[k] = push(group.at[s], group.at[slot_of[(k, 1)]], f_send.at[k], f_recv.at[k], 0, 1)

    pl.semaphore_wait(barrier, peers - 1)
    for k in far:
        q_copies[k].start()
    f_copies[0].start()

    unit[pl.ds(n, 8), :] = jnp.zeros((8, unit.shape[1]), F32)

    def forward(i, c):
        at = pl.ds(pl.multiple_of(i * TILE, TILE), TILE)
        unit[at, :] = tower(table[at, :], w1[...], w2[...])[3]
        return c

    lax.fori_loop(0, n // TILE, forward, 0)

    def span(t):
        return pl.ds(pl.multiple_of(t * cap, cap), cap)

    def gather_list(t):
        for j in range(cap):
            wide[pl.ds(t * cap + j, 1), :] = unit[pl.ds(rows[j, t], 1), :]
        send[span(t), :] = wide[span(t), :].astype(BF16)

    def send_list(k, c):
        t = lax.rem(me + k, peers)
        gather_list(t)
        pltpu.make_async_remote_copy(
            src_ref=send.at[span(t), :], dst_ref=recv.at[span(me), :],
            send_sem=a_send, recv_sem=a_recv, device_id=place(t), device_id_type=MESH,
        ).start()
        return c

    index.wait()
    lax.fori_loop(1, peers, send_list, 0)
    gather_list(me)
    keep = pltpu.make_async_copy(send.at[span(me), :], recv.at[span(me), :], l_sem)
    keep.start()
    for k in far:
        q_copies[k].wait_recv()
        f_copies[k].start()

    for i in range(n // TILE):
        at = pl.ds(i * TILE, TILE)
        pre, sig, inv, _ = tower(table[at, :], w1[...], w2[...])
        pexp[i, :, :512] = (sig * (1.0 + pre * (1.0 - sig)) * inv).astype(BF16)
        o_copies.append(
            pltpu.make_async_copy(pexp.at[i, :, pl.ds(0, 512)], slopes.at[at, :], o_sem.at[i])
        )
        o_copies[-1].start()

    low_part = jnp.transpose(live_rows[...].astype(F32))
    high_part = jnp.floor(low_part * (1.0 / 64.0))
    low_part = low_part - 64.0 * high_part
    width = peers // GROUPS * cap
    tiled = (
        lax.broadcasted_iota(jnp.int32, (cap, width), 0)
        == lax.rem(lax.broadcasted_iota(jnp.int32, (cap, width), 1), cap)
    ).astype(F32).astype(BF16)
    along = 64.0 * mm(high_part.astype(BF16), tiled) + mm(low_part.astype(BF16), tiled)
    mine = lax.rem(
        lax.broadcasted_iota(jnp.int32, along.shape, 0), peers // GROUPS
    ) == lax.broadcasted_iota(jnp.int32, along.shape, 1) // cap
    along = jnp.where(mine, along, 0.0)
    for b in range(GROUPS):
        part = along[b * (peers // GROUPS):(b + 1) * (peers // GROUPS), :]
        row_at[b:b + 1, :] = jnp.sum(part, axis=0, keepdims=True).astype(jnp.int32)

    keep.wait()
    others = pl.ds(0, (peers - 1) * cap)
    pltpu.make_async_copy(send.at[others, :], recv.at[others, :], a_recv).wait()
    wide[...] = recv[...].astype(F32)

    def pick(i, c):
        for j in range(32):
            low[pl.ds(i * 32 + j, 1), :] = wide[pl.ds(neg_slot[i * 32 + j], 1), :]
        for j in range(32):
            low[pl.ds(users + i * 32 + j, 1), :] = wide[pl.ds(pos_slot[i * 32 + j], 1), :]
        return c

    lax.fori_loop(0, users // 32, pick, 0)
    cols[...] = low[pl.ds(0, 2 * users), :].astype(BF16)

    for c in o_copies:
        c.wait()
    s_copies = []

    def compute(first, last):
        def one(k, c):
            s = mm_t(cols[pl.ds(users, users), :], group[k])
            e = jnp.exp2(s * (LOGIT_SCALE * LOG2E))
            pexp[k] = e.astype(BF16)
            sums_out[k] = jnp.sum(e, axis=0, keepdims=True)
            return c

        lax.fori_loop(first, last, one, 0)
        for i in range(first, last):
            k, flip = names[i]
            b = slot_of[((chips - k) % chips, flip)]
            s_copies.append(push(sums_out.at[i], sums_in.at[b], s_send.at[i], s_recv.at[b], k, flip))
            s_copies[-1].start()

    for c in f_copies.values():
        c.wait_recv()
    compute(1, 5)
    compute(5, grp)

    s = mm_t(cols[pl.ds(0, users), :], group[0])
    e = jnp.exp2(s * (LOGIT_SCALE * LOG2E))
    nexp[...] = e.astype(BF16)
    other = jnp.sum(e, axis=0, keepdims=True)
    s = mm_t(cols[pl.ds(users, users), :], group[0])
    hit = lax.broadcasted_iota(jnp.int32, s.shape, 0) == lax.broadcasted_iota(jnp.int32, s.shape, 1)
    e = jnp.where(hit, 0.0, jnp.exp2(s * (LOGIT_SCALE * LOG2E)))
    own_score = jnp.sum(jnp.where(hit, s, 0.0), axis=0, keepdims=True) * LOGIT_SCALE
    pexp[0] = e.astype(BF16)
    other = other + jnp.sum(e, axis=0, keepdims=True)

    for c in s_copies:
        c.wait_recv()

    for k in range(1, grp):
        other = other + sums_in[k]
    total = other + jnp.exp2(own_score * LOG2E)
    loss[...] = jnp.log(total) - own_score
    rate = LOGIT_SCALE / total
    rates[0] = rate
    r_copies = []
    for i in range(1, grp):
        k, flip = names[i]
        b = slot_of[((chips - k) % chips, flip)]
        r_copies.append(push(rates.at[0], rates.at[b], r_send.at[i], r_recv.at[b], k, flip))
        r_copies[-1].start()

    scaled[0] = (group[0].astype(F32) * upright(rate)).astype(BF16)
    acc[...] = spread(neg_at[...], mm(nexp[...], scaled[0]))
    own = group[0].astype(F32) * upright(rate * other)
    for c in r_copies:
        c.wait_recv()

    def scale(k, c):
        scaled[k] = (group[k].astype(F32) * upright(rates[k])).astype(BF16)
        return c

    lax.fori_loop(1, grp, scale, 0)
    grads = mm(pexp[0], scaled[0]) - own
    for k in range(1, grp):
        grads = grads + mm(pexp[k], scaled[k])
    total_grads = acc[...] + spread(pos_at[...], grads)
    half = n // 2
    back_send[pl.ds(0, half), :] = total_grads[:, :128].astype(BF16)
    back_send[pl.ds(half, half), :] = total_grads[:, 128:].astype(BF16)

    per = peers // GROUPS

    def send_back(k, c):
        t = lax.rem(me + k, peers)
        pltpu.make_async_remote_copy(
            src_ref=back_send.at[span(t), :], dst_ref=back_recv.at[span(me), :],
            send_sem=b_send, recv_sem=b_recv.at[me // per], device_id=place(t), device_id_type=MESH,
        ).start()
        return c

    lax.fori_loop(1, peers, send_back, 0)
    keep = pltpu.make_async_copy(
        back_send.at[span(me), :], back_recv.at[span(me), :], b_recv.at[me // per]
    )
    keep.start()

    acc[...] = jnp.zeros(acc.shape, F32)

    def arrive(i, c):
        b = lax.rem(me // per + 2 * GROUPS - 1 - i, GROUPS)
        at = pl.ds(pl.multiple_of(b * (per * cap), per * cap), per * cap)
        pltpu.make_async_copy(back_send.at[at, :], back_recv.at[at, :], b_recv.at[b]).wait()
        acc[...] = acc[...] + spread(row_at[pl.ds(b, 1), :], back_recv[at, :])
        return c

    lax.fori_loop(0, GROUPS, arrive, 0)

    for i in range(n // TILE):
        at = pl.ds(i * TILE, TILE)
        side = i * TILE // half * 128
        grad = acc[pl.ds(i * TILE % half, TILE), side:side + 128]
        u = unit[at, :]
        d_out[at, :] = (grad - u * jnp.sum(u * grad, axis=-1, keepdims=True)).astype(BF16)

    for c in list(q_copies.values()) + list(f_copies.values()) + s_copies + r_copies:
        c.wait_send()
    pltpu.make_async_copy(send.at[others, :], recv.at[others, :], a_send).wait()
    pltpu.make_async_copy(back_send.at[others, :], back_recv.at[others, :], b_send).wait()


def row_kernel(d_out, slopes, w1, w2, out):
    d_pre = (mm_t(d_out[...], w2[...]) * slopes[...].astype(F32)).astype(BF16)
    out[...] = mm_t(d_pre, w1[...])


def per_device(
    item_table, send_rows, send_count, pos_slot, neg_slot, user_ids,
    user_table, item_w1, item_w2, user_w1, user_w2,
):
    peers, cap = send_rows.shape[1:]
    slots = peers * cap
    n, users = item_table.shape[0], pos_slot.shape[0]
    vocab, outw = user_table.shape[0], item_w2.shape[1]
    grp = lax.axis_size("grp")
    chips = grp // 2
    neg = neg_slot.reshape(-1)

    dma = pltpu.SemaphoreType.DMA
    vm = pltpu.VMEM
    d_out, slopes, loss = pl.pallas_call(
        window_kernel,
        out_shape=[
            jax.ShapeDtypeStruct((n, outw), BF16),
            jax.ShapeDtypeStruct((n, item_w1.shape[1]), BF16),
            jax.ShapeDtypeStruct((1, users), F32),
        ],
        in_specs=[SMEM] * 3 + [VMEM] * 9 + [ANY],
        out_specs=[VMEM, ANY, VMEM],
        scratch_shapes=[
            vm(user_table.shape, BF16), vm((vocab, 128), F32), vm((vocab, 128), F32),
            vm((users, 128), F32), vm((users, 128), F32),
            vm((n + 8, outw), F32), vm((slots, outw), F32),
            vm((slots, outw), BF16), vm((slots, outw), BF16),
            vm((2 * users, outw), BF16),
            vm((grp, users, outw), BF16), vm((grp, users, users), BF16), vm((users, users), BF16),
            vm((grp, users, outw), BF16),
            vm((grp, 1, users), F32), vm((grp, 1, users), F32), vm((grp, 1, users), F32),
            vm((n // 2, 2 * outw), F32),
            vm((slots, outw), BF16), vm((slots, outw), BF16),
            vm((cap, peers), jnp.int32), pltpu.SMEM((cap, peers), jnp.int32),
            vm((GROUPS, slots // GROUPS), jnp.int32),
            dma, dma, dma((n // TILE,)), dma, dma, dma, dma((GROUPS,)), dma,
            dma((chips,)), dma((chips,)), dma((chips,)), dma((chips,)),
            dma((grp,)), dma((grp,)), dma((grp,)), dma((grp,)),
        ],
        compiler_params=pltpu.CompilerParams(
            collective_id=0, has_side_effects=True, vmem_limit_bytes=60 * 2**20
        ),
        cost_estimate=pl.CostEstimate(flops=2**34, bytes_accessed=2**24, transcendentals=2**24),
        name="window",
    )(
        pos_slot, neg, user_ids.T, send_rows[0].T, send_count, item_table, item_w1, item_w2,
        user_w1, user_w2, pos_slot.reshape(1, -1), neg_slot, user_table,
    )
    block = 512
    table_grad = pl.pallas_call(
        row_kernel,
        out_shape=jax.ShapeDtypeStruct(item_table.shape, F32),
        grid=(n // block,),
        in_specs=[
            pl.BlockSpec((block, outw), lambda i: (i, 0)),
            pl.BlockSpec((block, item_w1.shape[1]), lambda i: (i, 0)),
            pl.BlockSpec(item_w1.shape, lambda i: (0, 0)),
            pl.BlockSpec(item_w2.shape, lambda i: (0, 0)),
        ],
        out_specs=pl.BlockSpec((block, item_table.shape[1]), lambda i: (i, 0)),
        compiler_params=pltpu.CompilerParams(vmem_limit_bytes=32 * 2**20),
        name="row_grads",
    )(d_out, slopes, item_w1, item_w2)
    return table_grad, loss.reshape(-1)


def solution(mesh):
    return jax.shard_map(
        per_device,
        mesh=mesh,
        in_specs=(
            P(("grp", "rep"), None),
            P(("grp", "rep"), None, None),
            P(("grp", "rep"), None),
            P(("grp", "rep")),
            P(("grp", "rep"), None),
            P(("grp", "rep"), None),
            P(), P(), P(), P(), P(),
        ),
        out_specs=(P(("grp", "rep"), None), P(("grp", "rep"))),
        check_vma=False,
    )
```

```python
import math

import jax
import jax.numpy as jnp
from jax import lax
from jax.experimental import pallas as pl
from jax.experimental.pallas import tpu as pltpu
from jax.sharding import PartitionSpec as P

LOGIT_SCALE = 20.0
NORM_EPS = 1e-06
LOG2E = math.log2(math.e)
MESH = pl.DeviceIdType.MESH
VMEM = pl.BlockSpec(memory_space=pltpu.VMEM)
SMEM = pl.BlockSpec(memory_space=pltpu.SMEM)
ANY = pl.BlockSpec(memory_space=pl.ANY)
F32, BF16 = jnp.float32, jnp.bfloat16
TILE = 1024
GROUPS = 8
PARTS = 4


def mm(a, b):
    return jnp.dot(a, b, preferred_element_type=F32)


def mm_t(a, b):
    return lax.dot_general(a, b, (((1,), (1,)), ((), ())), preferred_element_type=F32)


def tower(x, w1, w2):
    pre = mm(x, w1)
    sig = 0.5 + 0.5 * jnp.tanh(0.5 * pre)
    out = mm((pre * sig).astype(BF16), w2)
    inv = lax.rsqrt(jnp.sum(out * out, axis=-1, keepdims=True) + NORM_EPS)
    return pre, sig, inv, out * inv


def upright(row):
    return jnp.transpose(jnp.broadcast_to(row, (128, row.shape[1])))


def spread(at, grads):
    half = 2048
    low = jnp.where(at >= half, at - half, at)
    hot = jnp.where(
        lax.broadcasted_iota(jnp.int32, (half, at.shape[1]), 0) == low, 1.0, 0.0
    ).astype(BF16)
    upper = upright(at.astype(F32)) >= half
    grads = grads.astype(F32)
    both = jnp.concatenate(
        [jnp.where(upper, 0.0, grads), jnp.where(upper, grads, 0.0)], axis=1
    ).astype(BF16)
    return mm(hot, both)


def window_kernel(
    pos_slot, neg_slot, ids, lists, counts, table, w1, w2, u1, u2, pos_at, neg_at, user_table,
    d_out, slopes, loss,
    ut, low, high, plow, phigh, unit, wide, send, recv, cols, group, pexp, nexp, scaled,
    sums_out, sums_in, rates, acc, back_send, back_recv, live_rows, rows, row_at,
    t_sem, i_sem, o_sem, a_send, a_recv, b_send, b_recv, l_sem,
    q_send, q_recv, f_send, f_recv, s_send, s_recv, r_send, r_recv,
):
    n, users = table.shape[0], group.shape[1]
    cap = 32
    grp, rep = lax.axis_size("grp"), lax.axis_size("rep")
    peers = grp * rep
    chips = grp // 2
    g, r = lax.axis_index("grp"), lax.axis_index("rep")
    me = g * rep + r
    chip, core = g // 2, lax.rem(g, 2)

    def place(t):
        return (t // rep, lax.rem(t, rep))

    barrier = pltpu.get_barrier_semaphore()

    def greet(k, c):
        pl.semaphore_signal(
            barrier, inc=1, device_id=place(lax.rem(me + k, peers)), device_id_type=MESH
        )
        return c

    lax.fori_loop(1, peers, greet, 0)
    fetch = pltpu.make_async_copy(user_table, ut, t_sem)
    fetch.start()

    live = lax.broadcasted_iota(jnp.int32, lists.shape, 0) < counts[...]
    live_rows[...] = jnp.where(live, lists[...], n)
    index = pltpu.make_async_copy(live_rows, rows, i_sem)
    index.start()

    unit[pl.ds(n, 8), :] = jnp.zeros((8, unit.shape[1]), F32)

    def forward(i, c):
        at = pl.ds(pl.multiple_of(i * TILE, TILE), TILE)
        unit[at, :] = tower(table[at, :], w1[...], w2[...])[3]
        return c

    lax.fori_loop(0, n // TILE, forward, 0)

    fetch.wait()

    def widen(i, c):
        at = pl.ds(pl.multiple_of(i * 256, 256), 256)
        low[at, :] = ut[at, :128].astype(F32)
        high[at, :] = ut[at, 128:].astype(F32)
        return c

    lax.fori_loop(0, ut.shape[0] // 256, widen, 0)
    pl.semaphore_wait(barrier, peers - 1)

    def span(t):
        return pl.ds(pl.multiple_of(t * cap, cap), cap)

    def gather_list(t):
        for j in range(cap):
            wide[pl.ds(t * cap + j, 1), :] = unit[pl.ds(rows[j, t], 1), :]
        send[span(t), :] = wide[span(t), :].astype(BF16)

    def send_list(k, c):
        t = lax.rem(me + k, peers)
        gather_list(t)
        pltpu.make_async_remote_copy(
            src_ref=send.at[span(t), :], dst_ref=recv.at[span(me), :],
            send_sem=a_send, recv_sem=a_recv, device_id=place(t), device_id_type=MESH,
        ).start()
        return c

    index.wait()
    lax.fori_loop(1, peers, send_list, 0)
    gather_list(me)
    keep = pltpu.make_async_copy(send.at[span(me), :], recv.at[span(me), :], l_sem)
    keep.start()

    feat = ids.shape[0] // users

    def pool(i, c):
        for k in range(8):
            b = i * 8 + k
            at = [pl.ds(ids[b * feat + f], 1) for f in range(feat)]
            lo = [low[a, :] for a in at]
            hi = [high[a, :] for a in at]
            while len(lo) > 1:
                lo = [x + y for x, y in zip(lo[::2], lo[1::2])]
                hi = [x + y for x, y in zip(hi[::2], hi[1::2])]
            plow[pl.ds(b, 1), :] = lo[0]
            phigh[pl.ds(b, 1), :] = hi[0]
        return c

    far = sorted(range(1, chips), key=lambda k: (min(k, chips - k), k))
    names = [(0, 0), (0, 1)] + [(k, 0) for k in far] + [(k, 1) for k in far]
    slot_of = {name: i for i, name in enumerate(names)}

    def push(src, dst, ss, rs, k, flip):
        to = lax.rem(chip + k, chips) * 2 + (1 - core if flip else core)
        return pltpu.make_async_remote_copy(
            src_ref=src, dst_ref=dst, send_sem=ss, recv_sem=rs,
            device_id=(to, r), device_id_type=MESH,
        )

    quarter = users // PARTS

    def piece(slot, c):
        return group.at[slot, pl.ds(c * quarter, quarter), :]

    q_copies, f_copies = {}, {}
    for c in range(PARTS):
        f_copies[0, c] = push(piece(0, c), piece(1, c), f_send.at[c], f_recv.at[c], 0, 1)
        for k in far:
            s, at = slot_of[(k, 0)], k * PARTS + c
            q_copies[k, c] = push(
                piece(0, c), piece(s, c), q_send.at[at], q_recv.at[at], chips - k, 0
            )
            f_copies[k, c] = push(
                piece(s, c), piece(slot_of[(k, 1)], c), f_send.at[at], f_recv.at[at], 0, 1
            )

    def pass_on(c):
        for k in far:
            q_copies[k, c].wait_recv()
            f_copies[k, c].start()

    for c in range(PARTS):
        at = pl.ds(c * quarter, quarter)
        lax.fori_loop(c * (quarter // 8), (c + 1) * (quarter // 8), pool, 0)
        pooled = jnp.concatenate([plow[at, :], phigh[at, :]], axis=1).astype(BF16)
        group[0, at, :] = tower(pooled, u1[...], u2[...])[3].astype(BF16)
        for k in far:
            q_copies[k, c].start()
        f_copies[0, c].start()
        if c > 0:
            pass_on(c - 1)

    keep.wait()
    others = pl.ds(0, (peers - 1) * cap)
    pltpu.make_async_copy(send.at[others, :], recv.at[others, :], a_recv).wait()
    wide[...] = recv[...].astype(F32)

    def pick(i, c):
        for j in range(32):
            low[pl.ds(i * 32 + j, 1), :] = wide[pl.ds(neg_slot[i * 32 + j], 1), :]
        for j in range(32):
            low[pl.ds(users + i * 32 + j, 1), :] = wide[pl.ds(pos_slot[i * 32 + j], 1), :]
        return c

    lax.fori_loop(0, users // 32, pick, 0)
    cols[...] = low[pl.ds(0, 2 * users), :].astype(BF16)

    pass_on(PARTS - 1)
    s = mm_t(cols[pl.ds(0, users), :], group[0])
    e = jnp.exp2(s * (LOGIT_SCALE * LOG2E))
    nexp[...] = e.astype(BF16)
    neg_sum = jnp.sum(e, axis=0, keepdims=True)
    s_copies = []

    def compute(first, last):
        def one(k, c):
            s = mm_t(cols[pl.ds(users, users), :], group[k])
            e = jnp.exp2(s * (LOGIT_SCALE * LOG2E))
            pexp[k] = e.astype(BF16)
            sums_out[k] = jnp.sum(e, axis=0, keepdims=True)
            return c

        lax.fori_loop(first, last, one, 0)
        for i in range(first, last):
            k, flip = names[i]
            b = slot_of[((chips - k) % chips, flip)]
            s_copies.append(push(sums_out.at[i], sums_in.at[b], s_send.at[i], s_recv.at[b], k, flip))
            s_copies[-1].start()

    for c in f_copies.values():
        c.wait_recv()
    compute(1, 5)
    compute(5, grp)

    s = mm_t(cols[pl.ds(users, users), :], group[0])
    hit = lax.broadcasted_iota(jnp.int32, s.shape, 0) == lax.broadcasted_iota(jnp.int32, s.shape, 1)
    e = jnp.where(hit, 0.0, jnp.exp2(s * (LOGIT_SCALE * LOG2E)))
    own_score = jnp.sum(jnp.where(hit, s, 0.0), axis=0, keepdims=True) * LOGIT_SCALE
    pexp[0] = e.astype(BF16)
    other = neg_sum + jnp.sum(e, axis=0, keepdims=True)

    for c in s_copies:
        c.wait_recv()

    for k in range(1, grp):
        other = other + sums_in[k]
    total = other + jnp.exp2(own_score * LOG2E)
    loss[...] = jnp.log(total) - own_score
    rate = LOGIT_SCALE / total
    rates[0] = rate
    r_copies = []
    for i in range(1, grp):
        k, flip = names[i]
        b = slot_of[((chips - k) % chips, flip)]
        r_copies.append(push(rates.at[0], rates.at[b], r_send.at[i], r_recv.at[b], k, flip))
        r_copies[-1].start()

    scaled[0] = (group[0].astype(F32) * upright(rate)).astype(BF16)
    acc[...] = spread(neg_at[...], mm(nexp[...], scaled[0]))
    own = group[0].astype(F32) * upright(rate * other)
    for c in r_copies:
        c.wait_recv()

    def scale(k, c):
        scaled[k] = (group[k].astype(F32) * upright(rates[k])).astype(BF16)
        return c

    lax.fori_loop(1, grp, scale, 0)
    grads = mm(pexp[0], scaled[0]) - own
    for k in range(1, grp):
        grads = grads + mm(pexp[k], scaled[k])
    total_grads = acc[...] + spread(pos_at[...], grads)
    half = n // 2
    back_send[pl.ds(0, half), :] = total_grads[:, :128].astype(BF16)
    back_send[pl.ds(half, half), :] = total_grads[:, 128:].astype(BF16)

    per = peers // GROUPS

    def send_back(k, c):
        t = lax.rem(me + k, peers)
        pltpu.make_async_remote_copy(
            src_ref=back_send.at[span(t), :], dst_ref=back_recv.at[span(me), :],
            send_sem=b_send, recv_sem=b_recv.at[me // per], device_id=place(t), device_id_type=MESH,
        ).start()
        return c

    lax.fori_loop(1, peers, send_back, 0)
    keep = pltpu.make_async_copy(
        back_send.at[span(me), :], back_recv.at[span(me), :], b_recv.at[me // per]
    )
    keep.start()

    o_copies = []
    for i in range(n // TILE):
        at = pl.ds(i * TILE, TILE)
        pre, sig, inv, _ = tower(table[at, :], w1[...], w2[...])
        pexp[i, :, :512] = (sig * (1.0 + pre * (1.0 - sig)) * inv).astype(BF16)
        o_copies.append(
            pltpu.make_async_copy(pexp.at[i, :, pl.ds(0, 512)], slopes.at[at, :], o_sem.at[i])
        )
        o_copies[-1].start()

    low_part = jnp.transpose(live_rows[...].astype(F32))
    high_part = jnp.floor(low_part * (1.0 / 64.0))
    low_part = low_part - 64.0 * high_part
    width = peers // GROUPS * cap
    tiled = (
        lax.broadcasted_iota(jnp.int32, (cap, width), 0)
        == lax.rem(lax.broadcasted_iota(jnp.int32, (cap, width), 1), cap)
    ).astype(F32).astype(BF16)
    along = 64.0 * mm(high_part.astype(BF16), tiled) + mm(low_part.astype(BF16), tiled)
    mine = lax.rem(
        lax.broadcasted_iota(jnp.int32, along.shape, 0), peers // GROUPS
    ) == lax.broadcasted_iota(jnp.int32, along.shape, 1) // cap
    along = jnp.where(mine, along, 0.0)
    for b in range(GROUPS):
        part = along[b * (peers // GROUPS):(b + 1) * (peers // GROUPS), :]
        row_at[b:b + 1, :] = jnp.sum(part, axis=0, keepdims=True).astype(jnp.int32)

    acc[...] = jnp.zeros(acc.shape, F32)

    def arrive(i, c):
        b = lax.rem(me // per + 2 * GROUPS - 1 - i, GROUPS)
        at = pl.ds(pl.multiple_of(b * (per * cap), per * cap), per * cap)
        pltpu.make_async_copy(back_send.at[at, :], back_recv.at[at, :], b_recv.at[b]).wait()
        acc[...] = acc[...] + spread(row_at[pl.ds(b, 1), :], back_recv[at, :])
        return c

    lax.fori_loop(0, GROUPS, arrive, 0)

    for i in range(n // TILE):
        at = pl.ds(i * TILE, TILE)
        side = i * TILE // half * 128
        grad = acc[pl.ds(i * TILE % half, TILE), side:side + 128]
        u = unit[at, :]
        d_out[at, :] = (grad - u * jnp.sum(u * grad, axis=-1, keepdims=True)).astype(BF16)

    for c in list(q_copies.values()) + list(f_copies.values()) + s_copies + r_copies:
        c.wait_send()
    pltpu.make_async_copy(send.at[others, :], recv.at[others, :], a_send).wait()
    pltpu.make_async_copy(back_send.at[others, :], back_recv.at[others, :], b_send).wait()
    for c in o_copies:
        c.wait()


def row_kernel(d_out, slopes, w1, w2, out):
    d_pre = (mm_t(d_out[...], w2[...]) * slopes[...].astype(F32)).astype(BF16)
    out[...] = mm_t(d_pre, w1[...])


def per_device(
    item_table, send_rows, send_count, pos_slot, neg_slot, user_ids,
    user_table, item_w1, item_w2, user_w1, user_w2,
):
    peers, cap = send_rows.shape[1:]
    slots = peers * cap
    n, users = item_table.shape[0], pos_slot.shape[0]
    vocab, outw = user_table.shape[0], item_w2.shape[1]
    grp = lax.axis_size("grp")
    chips = grp // 2
    neg = neg_slot.reshape(-1)

    dma = pltpu.SemaphoreType.DMA
    vm = pltpu.VMEM
    d_out, slopes, loss = pl.pallas_call(
        window_kernel,
        out_shape=[
            jax.ShapeDtypeStruct((n, outw), BF16),
            jax.ShapeDtypeStruct((n, item_w1.shape[1]), BF16),
            jax.ShapeDtypeStruct((1, users), F32),
        ],
        in_specs=[SMEM] * 3 + [VMEM] * 9 + [ANY],
        out_specs=[VMEM, ANY, VMEM],
        scratch_shapes=[
            vm(user_table.shape, BF16), vm((vocab, 128), F32), vm((vocab, 128), F32),
            vm((users, 128), F32), vm((users, 128), F32),
            vm((n + 8, outw), F32), vm((slots, outw), F32),
            vm((slots, outw), BF16), vm((slots, outw), BF16),
            vm((2 * users, outw), BF16),
            vm((grp, users, outw), BF16), vm((grp, users, users), BF16), vm((users, users), BF16),
            vm((grp, users, outw), BF16),
            vm((grp, 1, users), F32), vm((grp, 1, users), F32), vm((grp, 1, users), F32),
            vm((n // 2, 2 * outw), F32),
            vm((slots, outw), BF16), vm((slots, outw), BF16),
            vm((cap, peers), jnp.int32), pltpu.SMEM((cap, peers), jnp.int32),
            vm((GROUPS, slots // GROUPS), jnp.int32),
            dma, dma, dma((n // TILE,)), dma, dma, dma, dma((GROUPS,)), dma,
            dma((chips * PARTS,)), dma((chips * PARTS,)), dma((chips * PARTS,)), dma((chips * PARTS,)),
            dma((grp,)), dma((grp,)), dma((grp,)), dma((grp,)),
        ],
        compiler_params=pltpu.CompilerParams(
            collective_id=0, has_side_effects=True, vmem_limit_bytes=60 * 2**20
        ),
        cost_estimate=pl.CostEstimate(flops=2**34, bytes_accessed=2**24, transcendentals=2**24),
        name="window",
    )(
        pos_slot, neg, user_ids.reshape(-1), send_rows[0].T, send_count, item_table, item_w1, item_w2,
        user_w1, user_w2, pos_slot.reshape(1, -1), neg_slot, user_table,
    )
    block = 1024
    table_grad = pl.pallas_call(
        row_kernel,
        out_shape=jax.ShapeDtypeStruct(item_table.shape, F32),
        grid=(n // block,),
        in_specs=[
            pl.BlockSpec((block, outw), lambda i: (i, 0)),
            pl.BlockSpec((block, item_w1.shape[1]), lambda i: (i, 0)),
            pl.BlockSpec(item_w1.shape, lambda i: (0, 0)),
            pl.BlockSpec(item_w2.shape, lambda i: (0, 0)),
        ],
        out_specs=pl.BlockSpec((block, item_table.shape[1]), lambda i: (i, 0)),
        compiler_params=pltpu.CompilerParams(vmem_limit_bytes=60 * 2**20),
        name="row_grads",
    )(d_out, slopes, item_w1, item_w2)
    return table_grad, loss.reshape(-1)


def solution(mesh):
    return jax.shard_map(
        per_device,
        mesh=mesh,
        in_specs=(
            P(("grp", "rep"), None),
            P(("grp", "rep"), None, None),
            P(("grp", "rep"), None),
            P(("grp", "rep")),
            P(("grp", "rep"), None),
            P(("grp", "rep"), None),
            P(), P(), P(), P(), P(),
        ),
        out_specs=(P(("grp", "rep"), None), P(("grp", "rep"))),
        check_vma=False,
    )
```

```python
import math

import jax
import jax.numpy as jnp
from jax import lax
from jax.experimental import pallas as pl
from jax.experimental.pallas import tpu as pltpu
from jax.sharding import PartitionSpec as P

LOGIT_SCALE = 20.0
NORM_EPS = 1e-06
LOG2E = math.log2(math.e)
MESH = pl.DeviceIdType.MESH
VMEM = pl.BlockSpec(memory_space=pltpu.VMEM)
SMEM = pl.BlockSpec(memory_space=pltpu.SMEM)
ANY = pl.BlockSpec(memory_space=pl.ANY)
F32, BF16 = jnp.float32, jnp.bfloat16
TILE = 1024
GROUPS = 8
PARTS = 4


def mm(a, b):
    return jnp.dot(a, b, preferred_element_type=F32)


def mm_t(a, b):
    return lax.dot_general(a, b, (((1,), (1,)), ((), ())), preferred_element_type=F32)


def tower(x, w1, w2):
    pre = mm(x, w1)
    sig = 0.5 + 0.5 * jnp.tanh(0.5 * pre)
    out = mm((pre * sig).astype(BF16), w2)
    inv = lax.rsqrt(jnp.sum(out * out, axis=-1, keepdims=True) + NORM_EPS)
    return pre, sig, inv, out * inv


def upright(row):
    return jnp.transpose(jnp.broadcast_to(row, (128, row.shape[1])))


def spread(at, grads):
    half = 2048
    low = jnp.where(at >= half, at - half, at)
    hot = jnp.where(
        lax.broadcasted_iota(jnp.int32, (half, at.shape[1]), 0) == low, 1.0, 0.0
    ).astype(BF16)
    upper = upright(at.astype(F32)) >= half
    grads = grads.astype(F32)
    both = jnp.concatenate(
        [jnp.where(upper, 0.0, grads), jnp.where(upper, grads, 0.0)], axis=1
    ).astype(BF16)
    return mm(hot, both)


def window_kernel(
    pos_slot, neg_slot, lists, id_rows, counts, table, w1, w2, u1, u2, pos_at, neg_at, user_table,
    d_out, slopes, loss,
    ut, low, high, plow, phigh, unit, wide, send, recv, cols, group, pexp, nexp, scaled,
    sums_out, sums_in, rates, acc, back_send, back_recv, live_rows, rows, row_at,
    ids, t_sem, i_sem, u_sem, o_sem, a_send, a_recv, b_send, b_recv, l_sem,
    q_send, q_recv, f_send, f_recv, s_send, s_recv, r_send, r_recv,
):
    n, users = table.shape[0], group.shape[1]
    cap = 32
    grp, rep = lax.axis_size("grp"), lax.axis_size("rep")
    peers = grp * rep
    chips = grp // 2
    g, r = lax.axis_index("grp"), lax.axis_index("rep")
    me = g * rep + r
    chip, core = g // 2, lax.rem(g, 2)

    def place(t):
        return (t // rep, lax.rem(t, rep))

    barrier = pltpu.get_barrier_semaphore()

    def greet(k, c):
        pl.semaphore_signal(
            barrier, inc=1, device_id=place(lax.rem(me + k, peers)), device_id_type=MESH
        )
        return c

    lax.fori_loop(1, peers, greet, 0)
    fetch = pltpu.make_async_copy(user_table, ut, t_sem)
    fetch.start()

    live = lax.broadcasted_iota(jnp.int32, lists.shape, 0) < counts[...]
    live_rows[...] = jnp.where(live, lists[...], n)
    index = pltpu.make_async_copy(live_rows, rows, i_sem)
    index.start()
    feat = id_rows.shape[0]
    u_copies = [
        pltpu.make_async_copy(id_rows.at[f], ids.at[pl.ds(f * users, users)], u_sem.at[f])
        for f in range(feat)
    ]
    for c in u_copies:
        c.start()

    unit[pl.ds(n, 8), :] = jnp.zeros((8, unit.shape[1]), F32)

    o_copies = []
    for i in range(n // TILE):
        at = pl.ds(i * TILE, TILE)
        pre, sig, inv, unit[at, :] = tower(table[at, :], w1[...], w2[...])
        pexp[i, :, :512] = (sig * (1.0 + pre * (1.0 - sig)) * inv).astype(BF16)
        o_copies.append(
            pltpu.make_async_copy(pexp.at[i, :, pl.ds(0, 512)], slopes.at[at, :], o_sem.at[i])
        )
        o_copies[-1].start()

    low_part = jnp.transpose(live_rows[...].astype(F32))
    high_part = jnp.floor(low_part * (1.0 / 64.0))
    low_part = low_part - 64.0 * high_part
    width = peers // GROUPS * cap
    tiled = (
        lax.broadcasted_iota(jnp.int32, (cap, width), 0)
        == lax.rem(lax.broadcasted_iota(jnp.int32, (cap, width), 1), cap)
    ).astype(F32).astype(BF16)
    along = 64.0 * mm(high_part.astype(BF16), tiled) + mm(low_part.astype(BF16), tiled)
    mine = lax.rem(
        lax.broadcasted_iota(jnp.int32, along.shape, 0), peers // GROUPS
    ) == lax.broadcasted_iota(jnp.int32, along.shape, 1) // cap
    along = jnp.where(mine, along, 0.0)
    for b in range(GROUPS):
        part = along[b * (peers // GROUPS):(b + 1) * (peers // GROUPS), :]
        row_at[b:b + 1, :] = jnp.sum(part, axis=0, keepdims=True).astype(jnp.int32)


    fetch.wait()

    def widen(i, c):
        at = pl.ds(pl.multiple_of(i * 256, 256), 256)
        low[at, :] = ut[at, :128].astype(F32)
        high[at, :] = ut[at, 128:].astype(F32)
        return c

    lax.fori_loop(0, ut.shape[0] // 256, widen, 0)
    pl.semaphore_wait(barrier, peers - 1)

    def span(t):
        return pl.ds(pl.multiple_of(t * cap, cap), cap)

    def gather_list(t):
        for j in range(cap):
            wide[pl.ds(t * cap + j, 1), :] = unit[pl.ds(rows[j, t], 1), :]
        send[span(t), :] = wide[span(t), :].astype(BF16)

    def send_list(k, c):
        t = lax.rem(me + k, peers)
        gather_list(t)
        pltpu.make_async_remote_copy(
            src_ref=send.at[span(t), :], dst_ref=recv.at[span(me), :],
            send_sem=a_send, recv_sem=a_recv, device_id=place(t), device_id_type=MESH,
        ).start()
        return c

    index.wait()
    lax.fori_loop(1, peers, send_list, 0)
    gather_list(me)
    keep = pltpu.make_async_copy(send.at[span(me), :], recv.at[span(me), :], l_sem)
    keep.start()

    for c in u_copies:
        c.wait()

    def pool(i, c):
        for k in range(8):
            b = i * 8 + k
            at = [pl.ds(ids[f * users + b], 1) for f in range(feat)]
            lo = [low[a, :] for a in at]
            hi = [high[a, :] for a in at]
            while len(lo) > 1:
                lo = [x + y for x, y in zip(lo[::2], lo[1::2])]
                hi = [x + y for x, y in zip(hi[::2], hi[1::2])]
            plow[pl.ds(b, 1), :] = lo[0]
            phigh[pl.ds(b, 1), :] = hi[0]
        return c

    far = sorted(range(1, chips), key=lambda k: (min(k, chips - k), k))
    names = [(0, 0), (0, 1)] + [(k, 0) for k in far] + [(k, 1) for k in far]
    slot_of = {name: i for i, name in enumerate(names)}

    def push(src, dst, ss, rs, k, flip):
        to = lax.rem(chip + k, chips) * 2 + (1 - core if flip else core)
        return pltpu.make_async_remote_copy(
            src_ref=src, dst_ref=dst, send_sem=ss, recv_sem=rs,
            device_id=(to, r), device_id_type=MESH,
        )

    quarter = users // PARTS

    def piece(slot, c):
        return group.at[slot, pl.ds(c * quarter, quarter), :]

    middle = 2 if chips == 4 else 0
    near = [k for k in far if k != middle]
    q_copies, f_copies = {}, {}
    for c in range(PARTS):
        f_copies[0, c] = push(piece(0, c), piece(1, c), f_send.at[c], f_recv.at[c], 0, 1)
        for k in far:
            s, at = slot_of[(k, 0)], k * PARTS + c
            src, to = 0, chips - k
            if k == middle:
                src, to = (slot_of[(1, 0)], chips - 1) if c % 2 == 0 else (slot_of[(chips - 1, 0)], 1)
            q_copies[k, c] = push(piece(src, c), piece(s, c), q_send.at[at], q_recv.at[at], to, 0)
            f_copies[k, c] = push(
                piece(s, c), piece(slot_of[(k, 1)], c), f_send.at[at], f_recv.at[at], 0, 1
            )

    def near_on(c):
        for k in near:
            q_copies[k, c].wait_recv()
            f_copies[k, c].start()
        if middle:
            q_copies[middle, c].start()

    def far_on(c):
        if middle:
            q_copies[middle, c].wait_recv()
            f_copies[middle, c].start()

    for c in range(PARTS):
        at = pl.ds(c * quarter, quarter)
        lax.fori_loop(c * (quarter // 8), (c + 1) * (quarter // 8), pool, 0)
        pooled = jnp.concatenate([plow[at, :], phigh[at, :]], axis=1).astype(BF16)
        group[0, at, :] = tower(pooled, u1[...], u2[...])[3].astype(BF16)
        for k in near:
            q_copies[k, c].start()
        f_copies[0, c].start()
        if c > 0:
            near_on(c - 1)
        if c > 1:
            far_on(c - 2)
    near_on(PARTS - 1)
    far_on(PARTS - 2)

    keep.wait()
    others = pl.ds(0, (peers - 1) * cap)
    pltpu.make_async_copy(send.at[others, :], recv.at[others, :], a_recv).wait()
    wide[...] = recv[...].astype(F32)

    def pick(i, c):
        for j in range(32):
            low[pl.ds(i * 32 + j, 1), :] = wide[pl.ds(neg_slot[i * 32 + j], 1), :]
        for j in range(32):
            low[pl.ds(users + i * 32 + j, 1), :] = wide[pl.ds(pos_slot[i * 32 + j], 1), :]
        return c

    lax.fori_loop(0, users // 32, pick, 0)
    cols[...] = low[pl.ds(0, 2 * users), :].astype(BF16)

    far_on(PARTS - 1)
    for c in o_copies:
        c.wait()
    s = mm_t(cols[pl.ds(0, users), :], group[0])
    e = jnp.exp2(s * (LOGIT_SCALE * LOG2E))
    nexp[...] = e.astype(BF16)
    neg_sum = jnp.sum(e, axis=0, keepdims=True)
    s_copies = []

    def compute(first, last):
        def one(k, c):
            s = mm_t(cols[pl.ds(users, users), :], group[k])
            e = jnp.exp2(s * (LOGIT_SCALE * LOG2E))
            pexp[k] = e.astype(BF16)
            sums_out[k] = jnp.sum(e, axis=0, keepdims=True)
            return c

        lax.fori_loop(first, last, one, 0)
        for i in range(first, last):
            k, flip = names[i]
            b = slot_of[((chips - k) % chips, flip)]
            s_copies.append(push(sums_out.at[i], sums_in.at[b], s_send.at[i], s_recv.at[b], k, flip))
            s_copies[-1].start()

    for c in f_copies.values():
        c.wait_recv()
    compute(1, 5)
    compute(5, grp)

    s = mm_t(cols[pl.ds(users, users), :], group[0])
    hit = lax.broadcasted_iota(jnp.int32, s.shape, 0) == lax.broadcasted_iota(jnp.int32, s.shape, 1)
    e = jnp.where(hit, 0.0, jnp.exp2(s * (LOGIT_SCALE * LOG2E)))
    own_score = jnp.sum(jnp.where(hit, s, 0.0), axis=0, keepdims=True) * LOGIT_SCALE
    pexp[0] = e.astype(BF16)
    other = neg_sum + jnp.sum(e, axis=0, keepdims=True)

    for c in s_copies:
        c.wait_recv()

    for k in range(1, grp):
        other = other + sums_in[k]
    total = other + jnp.exp2(own_score * LOG2E)
    loss[...] = jnp.log(total) - own_score
    rate = LOGIT_SCALE / total
    rates[0] = rate
    r_copies = []
    for i in range(1, grp):
        k, flip = names[i]
        b = slot_of[((chips - k) % chips, flip)]
        r_copies.append(push(rates.at[0], rates.at[b], r_send.at[i], r_recv.at[b], k, flip))
        r_copies[-1].start()

    scaled[0] = (group[0].astype(F32) * upright(rate)).astype(BF16)
    acc[...] = spread(neg_at[...], mm(nexp[...], scaled[0]))
    own = group[0].astype(F32) * upright(rate * other)
    for c in r_copies:
        c.wait_recv()

    def scale(k, c):
        scaled[k] = (group[k].astype(F32) * upright(rates[k])).astype(BF16)
        return c

    lax.fori_loop(1, grp, scale, 0)
    grads = mm(pexp[0], scaled[0]) - own
    for k in range(1, grp):
        grads = grads + mm(pexp[k], scaled[k])
    total_grads = acc[...] + spread(pos_at[...], grads)
    half = n // 2
    back_send[pl.ds(0, half), :] = total_grads[:, :128].astype(BF16)
    back_send[pl.ds(half, half), :] = total_grads[:, 128:].astype(BF16)

    per = peers // GROUPS

    def send_back(k, c):
        t = lax.rem(me + k, peers)
        pltpu.make_async_remote_copy(
            src_ref=back_send.at[span(t), :], dst_ref=back_recv.at[span(me), :],
            send_sem=b_send, recv_sem=b_recv.at[me // per], device_id=place(t), device_id_type=MESH,
        ).start()
        return c

    lax.fori_loop(1, peers, send_back, 0)
    keep = pltpu.make_async_copy(
        back_send.at[span(me), :], back_recv.at[span(me), :], b_recv.at[me // per]
    )
    keep.start()

    acc[...] = jnp.zeros(acc.shape, F32)

    def arrive(i, c):
        b = lax.rem(me // per + 2 * GROUPS - 1 - i, GROUPS)
        at = pl.ds(pl.multiple_of(b * (per * cap), per * cap), per * cap)
        pltpu.make_async_copy(back_send.at[at, :], back_recv.at[at, :], b_recv.at[b]).wait()
        acc[...] = acc[...] + spread(row_at[pl.ds(b, 1), :], back_recv[at, :])
        return c

    lax.fori_loop(0, GROUPS, arrive, 0)

    for i in range(n // TILE):
        at = pl.ds(i * TILE, TILE)
        side = i * TILE // half * 128
        grad = acc[pl.ds(i * TILE % half, TILE), side:side + 128]
        u = unit[at, :]
        d_out[at, :] = (grad - u * jnp.sum(u * grad, axis=-1, keepdims=True)).astype(BF16)

    for c in list(q_copies.values()) + list(f_copies.values()) + s_copies + r_copies:
        c.wait_send()
    pltpu.make_async_copy(send.at[others, :], recv.at[others, :], a_send).wait()
    pltpu.make_async_copy(back_send.at[others, :], back_recv.at[others, :], b_send).wait()


def row_kernel(d_out, slopes, w1, w2, loss_in, out, loss):
    loss[...] = loss_in[...]
    d_pre = (mm_t(d_out[...], w2[...]) * slopes[...].astype(F32)).astype(BF16)
    out[...] = mm_t(d_pre, w1[...])


def per_device(
    item_table, send_rows, send_count, pos_slot, neg_slot, user_ids,
    user_table, item_w1, item_w2, user_w1, user_w2,
):
    peers, cap = send_rows.shape[1:]
    slots = peers * cap
    n, users = item_table.shape[0], pos_slot.shape[0]
    vocab, outw = user_table.shape[0], item_w2.shape[1]
    grp = lax.axis_size("grp")
    chips = grp // 2
    neg = neg_slot.reshape(-1)

    dma = pltpu.SemaphoreType.DMA
    vm = pltpu.VMEM
    d_out, slopes, loss = pl.pallas_call(
        window_kernel,
        out_shape=[
            jax.ShapeDtypeStruct((n, outw), BF16),
            jax.ShapeDtypeStruct((n, item_w1.shape[1]), BF16),
            jax.ShapeDtypeStruct((1, users), F32),
        ],
        in_specs=[SMEM] * 2 + [VMEM] * 10 + [ANY],
        out_specs=[VMEM, ANY, VMEM],
        scratch_shapes=[
            vm(user_table.shape, BF16), vm((vocab, 128), F32), vm((vocab, 128), F32),
            vm((users, 128), F32), vm((users, 128), F32),
            vm((n + 8, outw), F32), vm((slots, outw), F32),
            vm((slots, outw), BF16), vm((slots, outw), BF16),
            vm((2 * users, outw), BF16),
            vm((grp, users, outw), BF16), vm((grp, users, users), BF16), vm((users, users), BF16),
            vm((grp, users, outw), BF16),
            vm((grp, 1, users), F32), vm((grp, 1, users), F32), vm((grp, 1, users), F32),
            vm((n // 2, 2 * outw), F32),
            vm((slots, outw), BF16), vm((slots, outw), BF16),
            vm((cap, peers), jnp.int32), pltpu.SMEM((cap, peers), jnp.int32),
            vm((GROUPS, slots // GROUPS), jnp.int32),
            pltpu.SMEM((user_ids.size,), jnp.int32),
            dma, dma, dma((user_ids.shape[1],)), dma((n // TILE,)), dma, dma, dma, dma((GROUPS,)), dma,
            dma((chips * PARTS,)), dma((chips * PARTS,)), dma((chips * PARTS,)), dma((chips * PARTS,)),
            dma((grp,)), dma((grp,)), dma((grp,)), dma((grp,)),
        ],
        compiler_params=pltpu.CompilerParams(
            collective_id=0, has_side_effects=True, vmem_limit_bytes=60 * 2**20
        ),
        cost_estimate=pl.CostEstimate(flops=2**34, bytes_accessed=2**24, transcendentals=2**24),
        name="window",
    )(
        pos_slot, neg, send_rows[0].T, user_ids.T, send_count, item_table, item_w1, item_w2,
        user_w1, user_w2, pos_slot.reshape(1, -1), neg_slot, user_table,
    )
    block = 512
    table_grad, loss = pl.pallas_call(
        row_kernel,
        out_shape=[
            jax.ShapeDtypeStruct(item_table.shape, F32),
            jax.ShapeDtypeStruct((1, users), F32),
        ],
        grid=(n // block,),
        in_specs=[
            pl.BlockSpec((block, outw), lambda i: (i, 0)),
            pl.BlockSpec((block, item_w1.shape[1]), lambda i: (i, 0)),
            pl.BlockSpec(item_w1.shape, lambda i: (0, 0)),
            pl.BlockSpec(item_w2.shape, lambda i: (0, 0)),
            pl.BlockSpec((1, users), lambda i: (0, 0)),
        ],
        out_specs=[
            pl.BlockSpec((block, item_table.shape[1]), lambda i: (i, 0)),
            pl.BlockSpec((1, users), lambda i: (0, 0)),
        ],
        compiler_params=pltpu.CompilerParams(vmem_limit_bytes=60 * 2**20),
        name="row_grads",
    )(d_out, slopes, item_w1, item_w2, loss)
    return table_grad, loss.reshape(-1)


def solution(mesh):
    return jax.shard_map(
        per_device,
        mesh=mesh,
        in_specs=(
            P(("grp", "rep"), None),
            P(("grp", "rep"), None, None),
            P(("grp", "rep"), None),
            P(("grp", "rep")),
            P(("grp", "rep"), None),
            P(("grp", "rep"), None),
            P(), P(), P(), P(), P(),
        ),
        out_specs=(P(("grp", "rep"), None), P(("grp", "rep"))),
        check_vma=False,
    )
```

```python
import math

import jax
import jax.numpy as jnp
from jax import lax
from jax.experimental import pallas as pl
from jax.experimental.pallas import tpu as pltpu
from jax.sharding import PartitionSpec as P

LOGIT_SCALE = 20.0
NORM_EPS = 1e-06
LOG2E = math.log2(math.e)
MESH = pl.DeviceIdType.MESH
VMEM = pl.BlockSpec(memory_space=pltpu.VMEM)
SMEM = pl.BlockSpec(memory_space=pltpu.SMEM)
ANY = pl.BlockSpec(memory_space=pl.ANY)
F32, BF16 = jnp.float32, jnp.bfloat16
TILE = 1024
GROUPS = 8
PARTS = 4


def mm(a, b):
    return jnp.dot(a, b, preferred_element_type=F32)


def mm_t(a, b):
    return lax.dot_general(a, b, (((1,), (1,)), ((), ())), preferred_element_type=F32)


def tower(x, w1, w2):
    pre = mm(x, w1)
    sig = 0.5 + 0.5 * jnp.tanh(0.5 * pre)
    out = mm((pre * sig).astype(BF16), w2)
    inv = lax.rsqrt(jnp.sum(out * out, axis=-1, keepdims=True) + NORM_EPS)
    return pre, sig, inv, out * inv


def upright(row):
    return jnp.transpose(jnp.broadcast_to(row, (128, row.shape[1])))


def spread(at, grads):
    half = 2048
    low = jnp.where(at >= half, at - half, at)
    hot = jnp.where(
        lax.broadcasted_iota(jnp.int32, (half, at.shape[1]), 0) == low, 1.0, 0.0
    ).astype(BF16)
    upper = upright(at.astype(F32)) >= half
    grads = grads.astype(F32)
    both = jnp.concatenate(
        [jnp.where(upper, 0.0, grads), jnp.where(upper, grads, 0.0)], axis=1
    ).astype(BF16)
    return mm(hot, both)


def window_kernel(
    pos_slot, neg_slot, lists, id_rows, counts, table, w1, w2, u1, u2, pos_at, neg_at, user_table,
    d_out, slopes, loss,
    ut, low, high, plow, phigh, unit, wide, send, recv, cols, group, pexp, nexp, scaled,
    sums_out, sums_in, rates, acc, back_send, back_recv, live_rows, rows, row_at,
    ids, meet, t_sem, i_sem, u_sem, o_sem, a_send, a_recv, b_send, b_recv, l_sem,
    q_send, q_recv, f_send, f_recv, s_send, s_recv, r_send, r_recv,
):
    n, users = table.shape[0], group.shape[1]
    cap = 32
    grp, rep = lax.axis_size("grp"), lax.axis_size("rep")
    peers = grp * rep
    chips = grp // 2
    g, r = lax.axis_index("grp"), lax.axis_index("rep")
    me = g * rep + r
    chip, core = g // 2, lax.rem(g, 2)

    def place(t):
        return (t // rep, lax.rem(t, rep))

    barrier = pltpu.get_barrier_semaphore()

    def greet(sem, to):
        pl.semaphore_signal(sem, inc=1, device_id=to, device_id_type=MESH)

    def greet_grp(k, c):
        greet(barrier, (lax.rem(g + k, grp), r))
        return c

    def greet_rep(k, c):
        greet(barrier, (g, lax.rem(r + k, rep)))
        return c

    def greet_again(k, c):
        greet(meet, (g, lax.rem(r + k, rep)))
        return c

    lax.fori_loop(1, grp, greet_grp, 0)
    lax.fori_loop(1, rep, greet_rep, 0)
    fetch = pltpu.make_async_copy(user_table, ut, t_sem)
    fetch.start()

    live = lax.broadcasted_iota(jnp.int32, lists.shape, 0) < counts[...]
    live_rows[...] = jnp.where(live, lists[...], n)
    index = pltpu.make_async_copy(live_rows, rows, i_sem)
    index.start()
    feat = id_rows.shape[0]
    u_copies = [
        pltpu.make_async_copy(id_rows.at[f], ids.at[pl.ds(f * users, users)], u_sem.at[f])
        for f in range(feat)
    ]
    for c in u_copies:
        c.start()

    unit[pl.ds(n, 8), :] = jnp.zeros((8, unit.shape[1]), F32)

    o_copies = []
    for i in range(n // TILE):
        at = pl.ds(i * TILE, TILE)
        pre, sig, inv, unit[at, :] = tower(table[at, :], w1[...], w2[...])
        pexp[i, :, :512] = (sig * (1.0 + pre * (1.0 - sig)) * inv).astype(BF16)
        o_copies.append(
            pltpu.make_async_copy(pexp.at[i, :, pl.ds(0, 512)], slopes.at[at, :], o_sem.at[i])
        )
        o_copies[-1].start()

    pl.semaphore_wait(barrier, grp + rep - 2)
    lax.fori_loop(1, rep, greet_again, 0)

    low_part = jnp.transpose(live_rows[...].astype(F32))
    high_part = jnp.floor(low_part * (1.0 / 64.0))
    low_part = low_part - 64.0 * high_part
    width = peers // GROUPS * cap
    tiled = (
        lax.broadcasted_iota(jnp.int32, (cap, width), 0)
        == lax.rem(lax.broadcasted_iota(jnp.int32, (cap, width), 1), cap)
    ).astype(F32).astype(BF16)
    along = 64.0 * mm(high_part.astype(BF16), tiled) + mm(low_part.astype(BF16), tiled)
    mine = lax.rem(
        lax.broadcasted_iota(jnp.int32, along.shape, 0), peers // GROUPS
    ) == lax.broadcasted_iota(jnp.int32, along.shape, 1) // cap
    along = jnp.where(mine, along, 0.0)
    for b in range(GROUPS):
        part = along[b * (peers // GROUPS):(b + 1) * (peers // GROUPS), :]
        row_at[b:b + 1, :] = jnp.sum(part, axis=0, keepdims=True).astype(jnp.int32)


    fetch.wait()

    def widen(i, c):
        at = pl.ds(pl.multiple_of(i * 256, 256), 256)
        low[at, :] = ut[at, :128].astype(F32)
        high[at, :] = ut[at, 128:].astype(F32)
        return c

    lax.fori_loop(0, ut.shape[0] // 256, widen, 0)
    pl.semaphore_wait(meet, rep - 1)

    def span(t):
        return pl.ds(pl.multiple_of(t * cap, cap), cap)

    def gather_list(t):
        for j in range(cap):
            wide[pl.ds(t * cap + j, 1), :] = unit[pl.ds(rows[j, t], 1), :]
        send[span(t), :] = wide[span(t), :].astype(BF16)

    def send_list(k, c):
        t = lax.rem(me + k, peers)
        gather_list(t)
        pltpu.make_async_remote_copy(
            src_ref=send.at[span(t), :], dst_ref=recv.at[span(me), :],
            send_sem=a_send, recv_sem=a_recv, device_id=place(t), device_id_type=MESH,
        ).start()
        return c

    index.wait()
    lax.fori_loop(1, peers, send_list, 0)
    gather_list(me)
    keep = pltpu.make_async_copy(send.at[span(me), :], recv.at[span(me), :], l_sem)
    keep.start()

    for c in u_copies:
        c.wait()

    def pool(i, c):
        for k in range(8):
            b = i * 8 + k
            at = [pl.ds(ids[f * users + b], 1) for f in range(feat)]
            lo = [low[a, :] for a in at]
            hi = [high[a, :] for a in at]
            while len(lo) > 1:
                lo = [x + y for x, y in zip(lo[::2], lo[1::2])]
                hi = [x + y for x, y in zip(hi[::2], hi[1::2])]
            plow[pl.ds(b, 1), :] = lo[0]
            phigh[pl.ds(b, 1), :] = hi[0]
        return c

    far = sorted(range(1, chips), key=lambda k: (min(k, chips - k), k))
    names = [(0, 0), (0, 1)] + [(k, 0) for k in far] + [(k, 1) for k in far]
    slot_of = {name: i for i, name in enumerate(names)}

    def push(src, dst, ss, rs, k, flip):
        to = lax.rem(chip + k, chips) * 2 + (1 - core if flip else core)
        return pltpu.make_async_remote_copy(
            src_ref=src, dst_ref=dst, send_sem=ss, recv_sem=rs,
            device_id=(to, r), device_id_type=MESH,
        )

    quarter = users // PARTS

    def piece(slot, c):
        return group.at[slot, pl.ds(c * quarter, quarter), :]

    middle = 2 if chips == 4 else 0
    near = [k for k in far if k != middle]
    q_copies, f_copies = {}, {}
    for c in range(PARTS):
        f_copies[0, c] = push(piece(0, c), piece(1, c), f_send.at[c], f_recv.at[c], 0, 1)
        for k in far:
            s, at = slot_of[(k, 0)], k * PARTS + c
            src, to = 0, chips - k
            if k == middle:
                src, to = (slot_of[(1, 0)], chips - 1) if c % 2 == 0 else (slot_of[(chips - 1, 0)], 1)
            q_copies[k, c] = push(piece(src, c), piece(s, c), q_send.at[at], q_recv.at[at], to, 0)
            f_copies[k, c] = push(
                piece(s, c), piece(slot_of[(k, 1)], c), f_send.at[at], f_recv.at[at], 0, 1
            )

    def near_on(c):
        for k in near:
            q_copies[k, c].wait_recv()
            f_copies[k, c].start()
        if middle:
            q_copies[middle, c].start()

    def far_on(c):
        if middle:
            q_copies[middle, c].wait_recv()
            f_copies[middle, c].start()

    for c in range(PARTS):
        at = pl.ds(c * quarter, quarter)
        lax.fori_loop(c * (quarter // 8), (c + 1) * (quarter // 8), pool, 0)
        pooled = jnp.concatenate([plow[at, :], phigh[at, :]], axis=1).astype(BF16)
        group[0, at, :] = tower(pooled, u1[...], u2[...])[3].astype(BF16)
        for k in near:
            q_copies[k, c].start()
        f_copies[0, c].start()
        if c > 0:
            near_on(c - 1)
        if c > 1:
            far_on(c - 2)
    near_on(PARTS - 1)
    far_on(PARTS - 2)

    keep.wait()
    others = pl.ds(0, (peers - 1) * cap)
    pltpu.make_async_copy(send.at[others, :], recv.at[others, :], a_recv).wait()
    wide[...] = recv[...].astype(F32)

    def pick(i, c):
        for j in range(32):
            low[pl.ds(i * 32 + j, 1), :] = wide[pl.ds(neg_slot[i * 32 + j], 1), :]
        for j in range(32):
            low[pl.ds(users + i * 32 + j, 1), :] = wide[pl.ds(pos_slot[i * 32 + j], 1), :]
        return c

    lax.fori_loop(0, users // 32, pick, 0)
    cols[...] = low[pl.ds(0, 2 * users), :].astype(BF16)

    far_on(PARTS - 1)
    for c in o_copies:
        c.wait()
    s = mm_t(cols[pl.ds(0, users), :], group[0])
    e = jnp.exp2(s * (LOGIT_SCALE * LOG2E))
    nexp[...] = e.astype(BF16)
    neg_sum = jnp.sum(e, axis=0, keepdims=True)
    s_copies = []

    def compute(first, last):
        def one(k, c):
            s = mm_t(cols[pl.ds(users, users), :], group[k])
            e = jnp.exp2(s * (LOGIT_SCALE * LOG2E))
            pexp[k] = e.astype(BF16)
            sums_out[k] = jnp.sum(e, axis=0, keepdims=True)
            return c

        lax.fori_loop(first, last, one, 0)
        for i in range(first, last):
            k, flip = names[i]
            b = slot_of[((chips - k) % chips, flip)]
            s_copies.append(push(sums_out.at[i], sums_in.at[b], s_send.at[i], s_recv.at[b], k, flip))
            s_copies[-1].start()

    for c in f_copies.values():
        c.wait_recv()
    compute(1, 5)
    compute(5, grp)

    s = mm_t(cols[pl.ds(users, users), :], group[0])
    hit = lax.broadcasted_iota(jnp.int32, s.shape, 0) == lax.broadcasted_iota(jnp.int32, s.shape, 1)
    e = jnp.where(hit, 0.0, jnp.exp2(s * (LOGIT_SCALE * LOG2E)))
    own_score = jnp.sum(jnp.where(hit, s, 0.0), axis=0, keepdims=True) * LOGIT_SCALE
    pexp[0] = e.astype(BF16)
    other = neg_sum + jnp.sum(e, axis=0, keepdims=True)

    for c in s_copies:
        c.wait_recv()

    for k in range(1, grp):
        other = other + sums_in[k]
    total = other + jnp.exp2(own_score * LOG2E)
    loss[...] = jnp.log(total) - own_score
    rate = LOGIT_SCALE / total
    rates[0] = rate
    r_copies = []
    for i in range(1, grp):
        k, flip = names[i]
        b = slot_of[((chips - k) % chips, flip)]
        r_copies.append(push(rates.at[0], rates.at[b], r_send.at[i], r_recv.at[b], k, flip))
        r_copies[-1].start()

    scaled[0] = (group[0].astype(F32) * upright(rate)).astype(BF16)
    acc[...] = spread(neg_at[...], mm(nexp[...], scaled[0]))
    own = group[0].astype(F32) * upright(rate * other)
    for c in r_copies:
        c.wait_recv()

    def scale(k, c):
        scaled[k] = (group[k].astype(F32) * upright(rates[k])).astype(BF16)
        return c

    lax.fori_loop(1, grp, scale, 0)
    grads = mm(pexp[0], scaled[0]) - own
    for k in range(1, grp):
        grads = grads + mm(pexp[k], scaled[k])
    total_grads = acc[...] + spread(pos_at[...], grads)
    half = n // 2
    back_send[pl.ds(0, half), :] = total_grads[:, :128].astype(BF16)
    back_send[pl.ds(half, half), :] = total_grads[:, 128:].astype(BF16)

    per = peers // GROUPS

    def send_back(k, c):
        t = lax.rem(me + k, peers)
        pltpu.make_async_remote_copy(
            src_ref=back_send.at[span(t), :], dst_ref=back_recv.at[span(me), :],
            send_sem=b_send, recv_sem=b_recv.at[me // per], device_id=place(t), device_id_type=MESH,
        ).start()
        return c

    lax.fori_loop(1, peers, send_back, 0)
    keep = pltpu.make_async_copy(
        back_send.at[span(me), :], back_recv.at[span(me), :], b_recv.at[me // per]
    )
    keep.start()

    acc[...] = jnp.zeros(acc.shape, F32)

    def arrive(i, c):
        b = lax.rem(me // per + 2 * GROUPS - 1 - i, GROUPS)
        at = pl.ds(pl.multiple_of(b * (per * cap), per * cap), per * cap)
        pltpu.make_async_copy(back_send.at[at, :], back_recv.at[at, :], b_recv.at[b]).wait()
        acc[...] = acc[...] + spread(row_at[pl.ds(b, 1), :], back_recv[at, :])
        return c

    lax.fori_loop(0, GROUPS, arrive, 0)

    for i in range(n // TILE):
        at = pl.ds(i * TILE, TILE)
        side = i * TILE // half * 128
        grad = acc[pl.ds(i * TILE % half, TILE), side:side + 128]
        u = unit[at, :]
        d_out[at, :] = (grad - u * jnp.sum(u * grad, axis=-1, keepdims=True)).astype(BF16)

    for c in list(q_copies.values()) + list(f_copies.values()) + s_copies + r_copies:
        c.wait_send()
    pltpu.make_async_copy(send.at[others, :], recv.at[others, :], a_send).wait()
    pltpu.make_async_copy(back_send.at[others, :], back_recv.at[others, :], b_send).wait()


def row_kernel(d_out, slopes, w1, w2, loss_in, out, loss):
    loss[...] = loss_in[...]
    d_pre = (mm_t(d_out[...], w2[...]) * slopes[...].astype(F32)).astype(BF16)
    out[...] = mm_t(d_pre, w1[...])


def per_device(
    item_table, send_rows, send_count, pos_slot, neg_slot, user_ids,
    user_table, item_w1, item_w2, user_w1, user_w2,
):
    peers, cap = send_rows.shape[1:]
    slots = peers * cap
    n, users = item_table.shape[0], pos_slot.shape[0]
    vocab, outw = user_table.shape[0], item_w2.shape[1]
    grp = lax.axis_size("grp")
    chips = grp // 2
    neg = neg_slot.reshape(-1)

    dma = pltpu.SemaphoreType.DMA
    vm = pltpu.VMEM
    d_out, slopes, loss = pl.pallas_call(
        window_kernel,
        out_shape=[
            jax.ShapeDtypeStruct((n, outw), BF16),
            jax.ShapeDtypeStruct((n, item_w1.shape[1]), BF16),
            jax.ShapeDtypeStruct((1, users), F32),
        ],
        in_specs=[SMEM] * 2 + [VMEM] * 10 + [ANY],
        out_specs=[VMEM, ANY, VMEM],
        scratch_shapes=[
            vm(user_table.shape, BF16), vm((vocab, 128), F32), vm((vocab, 128), F32),
            vm((users, 128), F32), vm((users, 128), F32),
            vm((n + 8, outw), F32), vm((slots, outw), F32),
            vm((slots, outw), BF16), vm((slots, outw), BF16),
            vm((2 * users, outw), BF16),
            vm((grp, users, outw), BF16), vm((grp, users, users), BF16), vm((users, users), BF16),
            vm((grp, users, outw), BF16),
            vm((grp, 1, users), F32), vm((grp, 1, users), F32), vm((grp, 1, users), F32),
            vm((n // 2, 2 * outw), F32),
            vm((slots, outw), BF16), vm((slots, outw), BF16),
            vm((cap, peers), jnp.int32), pltpu.SMEM((cap, peers), jnp.int32),
            vm((GROUPS, slots // GROUPS), jnp.int32),
            pltpu.SMEM((user_ids.size,), jnp.int32), pltpu.SemaphoreType.REGULAR,
            dma, dma, dma((user_ids.shape[1],)), dma((n // TILE,)), dma, dma, dma, dma((GROUPS,)), dma,
            dma((chips * PARTS,)), dma((chips * PARTS,)), dma((chips * PARTS,)), dma((chips * PARTS,)),
            dma((grp,)), dma((grp,)), dma((grp,)), dma((grp,)),
        ],
        compiler_params=pltpu.CompilerParams(
            collective_id=0, has_side_effects=True, vmem_limit_bytes=60 * 2**20
        ),
        cost_estimate=pl.CostEstimate(flops=2**34, bytes_accessed=2**24, transcendentals=2**24),
        name="window",
    )(
        pos_slot, neg, send_rows[0].T, user_ids.T, send_count, item_table, item_w1, item_w2,
        user_w1, user_w2, pos_slot.reshape(1, -1), neg_slot, user_table,
    )
    block = 1024
    table_grad, loss = pl.pallas_call(
        row_kernel,
        out_shape=[
            jax.ShapeDtypeStruct(item_table.shape, F32),
            jax.ShapeDtypeStruct((1, users), F32),
        ],
        grid=(n // block,),
        in_specs=[
            pl.BlockSpec((block, outw), lambda i: (i, 0)),
            pl.BlockSpec((block, item_w1.shape[1]), lambda i: (i, 0)),
            pl.BlockSpec(item_w1.shape, lambda i: (0, 0)),
            pl.BlockSpec(item_w2.shape, lambda i: (0, 0)),
            pl.BlockSpec((1, users), lambda i: (0, 0)),
        ],
        out_specs=[
            pl.BlockSpec((block, item_table.shape[1]), lambda i: (i, 0)),
            pl.BlockSpec((1, users), lambda i: (0, 0)),
        ],
        compiler_params=pltpu.CompilerParams(vmem_limit_bytes=60 * 2**20),
        name="row_grads",
    )(d_out, slopes, item_w1, item_w2, loss)
    return table_grad, loss.reshape(-1)


def solution(mesh):
    return jax.shard_map(
        per_device,
        mesh=mesh,
        in_specs=(
            P(("grp", "rep"), None),
            P(("grp", "rep"), None, None),
            P(("grp", "rep"), None),
            P(("grp", "rep")),
            P(("grp", "rep"), None),
            P(("grp", "rep"), None),
            P(), P(), P(), P(), P(),
        ),
        out_specs=(P(("grp", "rep"), None), P(("grp", "rep"))),
        check_vma=False,
    )
```

```python
import math

import jax
import jax.numpy as jnp
from jax import lax
from jax.experimental import pallas as pl
from jax.experimental.pallas import tpu as pltpu
from jax.sharding import PartitionSpec as P

LOGIT_SCALE = 20.0
NORM_EPS = 1e-06
LOG2E = math.log2(math.e)
MESH = pl.DeviceIdType.MESH
VMEM = pl.BlockSpec(memory_space=pltpu.VMEM)
SMEM = pl.BlockSpec(memory_space=pltpu.SMEM)
ANY = pl.BlockSpec(memory_space=pl.ANY)
F32, BF16 = jnp.float32, jnp.bfloat16
TILE = 1024
GROUPS = 8
PARTS = 4


def mm(a, b):
    return jnp.dot(a, b, preferred_element_type=F32)


def mm_t(a, b):
    return lax.dot_general(a, b, (((1,), (1,)), ((), ())), preferred_element_type=F32)


def tower(x, w1, w2):
    pre = mm(x, w1)
    sig = 0.5 + 0.5 * jnp.tanh(0.5 * pre)
    out = mm((pre * sig).astype(BF16), w2)
    inv = lax.rsqrt(jnp.sum(out * out, axis=-1, keepdims=True) + NORM_EPS)
    return pre, sig, inv, out * inv


def upright(row):
    return jnp.transpose(jnp.broadcast_to(row, (128, row.shape[1])))


def spread(at, grads):
    half = 2048
    low = jnp.where(at >= half, at - half, at)
    hot = jnp.where(
        lax.broadcasted_iota(jnp.int32, (half, at.shape[1]), 0) == low, 1.0, 0.0
    ).astype(BF16)
    upper = upright(at.astype(F32)) >= half
    grads = grads.astype(F32)
    both = jnp.concatenate(
        [jnp.where(upper, 0.0, grads), jnp.where(upper, grads, 0.0)], axis=1
    ).astype(BF16)
    return mm(hot, both)


def window_kernel(
    pos_slot, neg_slot, lists, id_rows, counts, table, w1, w2, u1, u2, pos_at, neg_at, user_table,
    d_out, slopes, loss,
    ut, low, high, plow, phigh, unit, wide, send, recv, cols, group, pexp, nexp, scaled,
    sums_out, sums_in, rates, acc, back_send, back_recv, live_rows, rows, row_at,
    ids, meet, t_sem, i_sem, u_sem, o_sem, a_send, a_recv, b_send, b_recv, l_sem,
    q_send, q_recv, f_send, f_recv, s_send, s_recv, r_send, r_recv,
):
    n, users = table.shape[0], group.shape[1]
    cap = 32
    grp, rep = lax.axis_size("grp"), lax.axis_size("rep")
    peers = grp * rep
    chips = grp // 2
    g, r = lax.axis_index("grp"), lax.axis_index("rep")
    me = g * rep + r
    chip, core = g // 2, lax.rem(g, 2)

    def place(t):
        return (t // rep, lax.rem(t, rep))

    barrier = pltpu.get_barrier_semaphore()

    def greet(sem, to):
        pl.semaphore_signal(sem, inc=1, device_id=to, device_id_type=MESH)

    def greet_grp(k, c):
        greet(barrier, (lax.rem(g + k, grp), r))
        return c

    def greet_rep(k, c):
        greet(barrier, (g, lax.rem(r + k, rep)))
        return c

    def greet_again(k, c):
        greet(meet, (g, lax.rem(r + k, rep)))
        return c

    lax.fori_loop(1, grp, greet_grp, 0)
    lax.fori_loop(1, rep, greet_rep, 0)
    fetch = pltpu.make_async_copy(user_table, ut, t_sem)
    fetch.start()

    live = lax.broadcasted_iota(jnp.int32, lists.shape, 0) < counts[...]
    live_rows[...] = jnp.where(live, lists[...], n)
    index = pltpu.make_async_copy(live_rows, rows, i_sem)
    index.start()
    feat = id_rows.shape[0]
    u_copies = [
        pltpu.make_async_copy(id_rows.at[f], ids.at[pl.ds(f * users, users)], u_sem.at[f])
        for f in range(feat)
    ]
    for c in u_copies:
        c.start()

    unit[pl.ds(n, 8), :] = jnp.zeros((8, unit.shape[1]), F32)

    o_copies = []
    for i in range(n // TILE):
        at = pl.ds(i * TILE, TILE)
        pre, sig, inv, unit[at, :] = tower(table[at, :], w1[...], w2[...])
        pexp[i, :, :512] = (sig * (1.0 + pre * (1.0 - sig)) * inv).astype(BF16)
        o_copies.append(
            pltpu.make_async_copy(pexp.at[i, :, pl.ds(0, 512)], slopes.at[at, :], o_sem.at[i])
        )
        o_copies[-1].start()

    pl.semaphore_wait(barrier, grp + rep - 2)
    lax.fori_loop(1, rep, greet_again, 0)

    low_part = jnp.transpose(live_rows[...].astype(F32))
    high_part = jnp.floor(low_part * (1.0 / 64.0))
    low_part = low_part - 64.0 * high_part
    width = peers // GROUPS * cap
    tiled = (
        lax.broadcasted_iota(jnp.int32, (cap, width), 0)
        == lax.rem(lax.broadcasted_iota(jnp.int32, (cap, width), 1), cap)
    ).astype(F32).astype(BF16)
    along = 64.0 * mm(high_part.astype(BF16), tiled) + mm(low_part.astype(BF16), tiled)
    mine = lax.rem(
        lax.broadcasted_iota(jnp.int32, along.shape, 0), peers // GROUPS
    ) == lax.broadcasted_iota(jnp.int32, along.shape, 1) // cap
    along = jnp.where(mine, along, 0.0)
    for b in range(GROUPS):
        part = along[b * (peers // GROUPS):(b + 1) * (peers // GROUPS), :]
        row_at[b:b + 1, :] = jnp.sum(part, axis=0, keepdims=True).astype(jnp.int32)


    fetch.wait()

    def widen(i, c):
        at = pl.ds(pl.multiple_of(i * 256, 256), 256)
        low[at, :] = ut[at, :128].astype(F32)
        high[at, :] = ut[at, 128:].astype(F32)
        return c

    lax.fori_loop(0, ut.shape[0] // 256, widen, 0)
    pl.semaphore_wait(meet, rep - 1)

    def span(t):
        return pl.ds(pl.multiple_of(t * cap, cap), cap)

    def gather_list(t):
        for j in range(cap):
            wide[pl.ds(t * cap + j, 1), :] = unit[pl.ds(rows[j, t], 1), :]
        send[span(t), :] = wide[span(t), :].astype(BF16)

    def send_lists(ks):
        ts = [lax.rem(me + k, peers) for k in ks]
        for t in ts:
            gather_list(t)
        for t in ts:
            pltpu.make_async_remote_copy(
                src_ref=send.at[span(t), :], dst_ref=recv.at[span(me), :],
                send_sem=a_send, recv_sem=a_recv, device_id=place(t), device_id_type=MESH,
            ).start()

    def send_pair(i, c):
        send_lists([2 * i + 1, 2 * i + 2])
        return c

    index.wait()
    lax.fori_loop(0, (peers - 1) // 2, send_pair, 0)
    send_lists([peers - 1])
    gather_list(me)
    keep = pltpu.make_async_copy(send.at[span(me), :], recv.at[span(me), :], l_sem)
    keep.start()

    for c in u_copies:
        c.wait()

    def pool(i, c):
        for k in range(16):
            b = i * 16 + k
            at = [pl.ds(ids[f * users + b], 1) for f in range(feat)]
            lo = [low[a, :] for a in at]
            hi = [high[a, :] for a in at]
            while len(lo) > 1:
                lo = [x + y for x, y in zip(lo[::2], lo[1::2])]
                hi = [x + y for x, y in zip(hi[::2], hi[1::2])]
            plow[pl.ds(b, 1), :] = lo[0]
            phigh[pl.ds(b, 1), :] = hi[0]
        return c

    far = sorted(range(1, chips), key=lambda k: (min(k, chips - k), k))
    names = [(0, 0), (0, 1)] + [(k, 0) for k in far] + [(k, 1) for k in far]
    slot_of = {name: i for i, name in enumerate(names)}

    def push(src, dst, ss, rs, k, flip):
        to = lax.rem(chip + k, chips) * 2 + (1 - core if flip else core)
        return pltpu.make_async_remote_copy(
            src_ref=src, dst_ref=dst, send_sem=ss, recv_sem=rs,
            device_id=(to, r), device_id_type=MESH,
        )

    quarter = users // PARTS

    def piece(slot, c):
        return group.at[slot, pl.ds(c * quarter, quarter), :]

    middle = 2 if chips == 4 else 0
    near = [k for k in far if k != middle]
    q_copies, f_copies = {}, {}
    for c in range(PARTS):
        f_copies[0, c] = push(piece(0, c), piece(1, c), f_send.at[c], f_recv.at[c], 0, 1)
        for k in far:
            s, at = slot_of[(k, 0)], k * PARTS + c
            src, to = 0, chips - k
            if k == middle:
                src, to = (slot_of[(1, 0)], chips - 1) if c % 2 == 0 else (slot_of[(chips - 1, 0)], 1)
            q_copies[k, c] = push(piece(src, c), piece(s, c), q_send.at[at], q_recv.at[at], to, 0)
            f_copies[k, c] = push(
                piece(s, c), piece(slot_of[(k, 1)], c), f_send.at[at], f_recv.at[at], 0, 1
            )

    def near_on(c):
        for k in near:
            q_copies[k, c].wait_recv()
            f_copies[k, c].start()
        if middle:
            q_copies[middle, c].start()

    def far_on(c):
        if middle:
            q_copies[middle, c].wait_recv()
            f_copies[middle, c].start()

    for c in range(PARTS):
        at = pl.ds(c * quarter, quarter)
        lax.fori_loop(c * (quarter // 16), (c + 1) * (quarter // 16), pool, 0)
        pooled = jnp.concatenate([plow[at, :], phigh[at, :]], axis=1).astype(BF16)
        group[0, at, :] = tower(pooled, u1[...], u2[...])[3].astype(BF16)
        for k in near:
            q_copies[k, c].start()
        f_copies[0, c].start()
        if c > 0:
            near_on(c - 1)
        if c > 1:
            far_on(c - 2)
    near_on(PARTS - 1)
    far_on(PARTS - 2)

    keep.wait()
    others = pl.ds(0, (peers - 1) * cap)
    pltpu.make_async_copy(send.at[others, :], recv.at[others, :], a_recv).wait()
    wide[...] = recv[...].astype(F32)

    def pick(i, c):
        for j in range(32):
            low[pl.ds(i * 32 + j, 1), :] = wide[pl.ds(neg_slot[i * 32 + j], 1), :]
        for j in range(32):
            low[pl.ds(users + i * 32 + j, 1), :] = wide[pl.ds(pos_slot[i * 32 + j], 1), :]
        return c

    lax.fori_loop(0, users // 32, pick, 0)
    cols[...] = low[pl.ds(0, 2 * users), :].astype(BF16)

    far_on(PARTS - 1)
    for c in o_copies:
        c.wait()
    s = mm_t(cols[pl.ds(0, users), :], group[0])
    e = jnp.exp2(s * (LOGIT_SCALE * LOG2E))
    nexp[...] = e.astype(BF16)
    neg_sum = jnp.sum(e, axis=0, keepdims=True)
    s_copies = []

    def compute(first, last):
        def one(k, c):
            s = mm_t(cols[pl.ds(users, users), :], group[k])
            e = jnp.exp2(s * (LOGIT_SCALE * LOG2E))
            pexp[k] = e.astype(BF16)
            sums_out[k] = jnp.sum(e, axis=0, keepdims=True)
            return c

        lax.fori_loop(first, last, one, 0)
        for i in range(first, last):
            k, flip = names[i]
            b = slot_of[((chips - k) % chips, flip)]
            s_copies.append(push(sums_out.at[i], sums_in.at[b], s_send.at[i], s_recv.at[b], k, flip))
            s_copies[-1].start()

    for c in f_copies.values():
        c.wait_recv()
    compute(1, 5)
    compute(5, grp)

    s = mm_t(cols[pl.ds(users, users), :], group[0])
    hit = lax.broadcasted_iota(jnp.int32, s.shape, 0) == lax.broadcasted_iota(jnp.int32, s.shape, 1)
    e = jnp.where(hit, 0.0, jnp.exp2(s * (LOGIT_SCALE * LOG2E)))
    own_score = jnp.sum(jnp.where(hit, s, 0.0), axis=0, keepdims=True) * LOGIT_SCALE
    pexp[0] = e.astype(BF16)
    other = neg_sum + jnp.sum(e, axis=0, keepdims=True)

    for c in s_copies:
        c.wait_recv()

    for k in range(1, grp):
        other = other + sums_in[k]
    total = other + jnp.exp2(own_score * LOG2E)
    loss[...] = jnp.log(total) - own_score
    rate = LOGIT_SCALE / total
    rates[0] = rate
    r_copies = []
    for i in range(1, grp):
        k, flip = names[i]
        b = slot_of[((chips - k) % chips, flip)]
        r_copies.append(push(rates.at[0], rates.at[b], r_send.at[i], r_recv.at[b], k, flip))
        r_copies[-1].start()

    scaled[0] = (group[0].astype(F32) * upright(rate)).astype(BF16)
    acc[...] = spread(neg_at[...], mm(nexp[...], scaled[0]))
    own = group[0].astype(F32) * upright(rate * other)
    for c in r_copies:
        c.wait_recv()

    def scale(k, c):
        scaled[k] = (group[k].astype(F32) * upright(rates[k])).astype(BF16)
        return c

    lax.fori_loop(1, grp, scale, 0)
    grads = mm(pexp[0], scaled[0]) - own
    for k in range(1, grp):
        grads = grads + mm(pexp[k], scaled[k])
    total_grads = acc[...] + spread(pos_at[...], grads)
    half = n // 2
    back_send[pl.ds(0, half), :] = total_grads[:, :128].astype(BF16)
    back_send[pl.ds(half, half), :] = total_grads[:, 128:].astype(BF16)

    per = peers // GROUPS

    def send_back(k, c):
        t = lax.rem(me + k, peers)
        pltpu.make_async_remote_copy(
            src_ref=back_send.at[span(t), :], dst_ref=back_recv.at[span(me), :],
            send_sem=b_send, recv_sem=b_recv.at[me // per], device_id=place(t), device_id_type=MESH,
        ).start()
        return c

    lax.fori_loop(1, peers, send_back, 0)
    keep = pltpu.make_async_copy(
        back_send.at[span(me), :], back_recv.at[span(me), :], b_recv.at[me // per]
    )
    keep.start()

    acc[...] = jnp.zeros(acc.shape, F32)

    def arrive(i, c):
        b = lax.rem(me // per + 2 * GROUPS - 1 - i, GROUPS)
        at = pl.ds(pl.multiple_of(b * (per * cap), per * cap), per * cap)
        pltpu.make_async_copy(back_send.at[at, :], back_recv.at[at, :], b_recv.at[b]).wait()
        acc[...] = acc[...] + spread(row_at[pl.ds(b, 1), :], back_recv[at, :])
        return c

    lax.fori_loop(0, GROUPS, arrive, 0)

    for i in range(n // TILE):
        at = pl.ds(i * TILE, TILE)
        side = i * TILE // half * 128
        grad = acc[pl.ds(i * TILE % half, TILE), side:side + 128]
        u = unit[at, :]
        d_out[at, :] = (grad - u * jnp.sum(u * grad, axis=-1, keepdims=True)).astype(BF16)

    for c in list(q_copies.values()) + list(f_copies.values()) + s_copies + r_copies:
        c.wait_send()
    pltpu.make_async_copy(send.at[others, :], recv.at[others, :], a_send).wait()
    pltpu.make_async_copy(back_send.at[others, :], back_recv.at[others, :], b_send).wait()


def row_kernel(d_out, slopes, w1, w2, loss_in, out, loss):
    loss[...] = loss_in[...]
    d_pre = (mm_t(d_out[...], w2[...]) * slopes[...].astype(F32)).astype(BF16)
    out[...] = mm_t(d_pre, w1[...])


def per_device(
    item_table, send_rows, send_count, pos_slot, neg_slot, user_ids,
    user_table, item_w1, item_w2, user_w1, user_w2,
):
    peers, cap = send_rows.shape[1:]
    slots = peers * cap
    n, users = item_table.shape[0], pos_slot.shape[0]
    vocab, outw = user_table.shape[0], item_w2.shape[1]
    grp = lax.axis_size("grp")
    chips = grp // 2
    neg = neg_slot.reshape(-1)

    dma = pltpu.SemaphoreType.DMA
    vm = pltpu.VMEM
    d_out, slopes, loss = pl.pallas_call(
        window_kernel,
        out_shape=[
            jax.ShapeDtypeStruct((n, outw), BF16),
            jax.ShapeDtypeStruct((n, item_w1.shape[1]), BF16),
            jax.ShapeDtypeStruct((1, users), F32),
        ],
        in_specs=[SMEM] * 2 + [VMEM] * 10 + [ANY],
        out_specs=[VMEM, ANY, VMEM],
        scratch_shapes=[
            vm(user_table.shape, BF16), vm((vocab, 128), F32), vm((vocab, 128), F32),
            vm((users, 128), F32), vm((users, 128), F32),
            vm((n + 8, outw), F32), vm((slots, outw), F32),
            vm((slots, outw), BF16), vm((slots, outw), BF16),
            vm((2 * users, outw), BF16),
            vm((grp, users, outw), BF16), vm((grp, users, users), BF16), vm((users, users), BF16),
            vm((grp, users, outw), BF16),
            vm((grp, 1, users), F32), vm((grp, 1, users), F32), vm((grp, 1, users), F32),
            vm((n // 2, 2 * outw), F32),
            vm((slots, outw), BF16), vm((slots, outw), BF16),
            vm((cap, peers), jnp.int32), pltpu.SMEM((cap, peers), jnp.int32),
            vm((GROUPS, slots // GROUPS), jnp.int32),
            pltpu.SMEM((user_ids.size,), jnp.int32), pltpu.SemaphoreType.REGULAR,
            dma, dma, dma((user_ids.shape[1],)), dma((n // TILE,)), dma, dma, dma, dma((GROUPS,)), dma,
            dma((chips * PARTS,)), dma((chips * PARTS,)), dma((chips * PARTS,)), dma((chips * PARTS,)),
            dma((grp,)), dma((grp,)), dma((grp,)), dma((grp,)),
        ],
        compiler_params=pltpu.CompilerParams(
            collective_id=0, has_side_effects=True, vmem_limit_bytes=60 * 2**20
        ),
        cost_estimate=pl.CostEstimate(flops=2**34, bytes_accessed=2**24, transcendentals=2**24),
        name="window",
    )(
        pos_slot, neg, send_rows[0].T, user_ids.T, send_count, item_table, item_w1, item_w2,
        user_w1, user_w2, pos_slot.reshape(1, -1), neg_slot, user_table,
    )
    block = 1024
    table_grad, loss = pl.pallas_call(
        row_kernel,
        out_shape=[
            jax.ShapeDtypeStruct(item_table.shape, F32),
            jax.ShapeDtypeStruct((1, users), F32),
        ],
        grid=(n // block,),
        in_specs=[
            pl.BlockSpec((block, outw), lambda i: (i, 0)),
            pl.BlockSpec((block, item_w1.shape[1]), lambda i: (i, 0)),
            pl.BlockSpec(item_w1.shape, lambda i: (0, 0)),
            pl.BlockSpec(item_w2.shape, lambda i: (0, 0)),
            pl.BlockSpec((1, users), lambda i: (0, 0)),
        ],
        out_specs=[
            pl.BlockSpec((block, item_table.shape[1]), lambda i: (i, 0)),
            pl.BlockSpec((1, users), lambda i: (0, 0)),
        ],
        compiler_params=pltpu.CompilerParams(vmem_limit_bytes=60 * 2**20),
        name="row_grads",
    )(d_out, slopes, item_w1, item_w2, loss)
    return table_grad, loss.reshape(-1)


def solution(mesh):
    return jax.shard_map(
        per_device,
        mesh=mesh,
        in_specs=(
            P(("grp", "rep"), None),
            P(("grp", "rep"), None, None),
            P(("grp", "rep"), None),
            P(("grp", "rep")),
            P(("grp", "rep"), None),
            P(("grp", "rep"), None),
            P(), P(), P(), P(), P(),
        ),
        out_specs=(P(("grp", "rep"), None), P(("grp", "rep"))),
        check_vma=False,
    )
```

```python
import math

import jax
import jax.numpy as jnp
from jax import lax
from jax.experimental import pallas as pl
from jax.experimental.pallas import tpu as pltpu
from jax.sharding import PartitionSpec as P

LOGIT_SCALE = 20.0
NORM_EPS = 1e-06
LOG2E = math.log2(math.e)
MESH = pl.DeviceIdType.MESH
VMEM = pl.BlockSpec(memory_space=pltpu.VMEM)
SMEM = pl.BlockSpec(memory_space=pltpu.SMEM)
ANY = pl.BlockSpec(memory_space=pl.ANY)
F32, BF16 = jnp.float32, jnp.bfloat16
TILE = 1024
GROUPS = 8
PARTS = 2


def mm(a, b):
    return jnp.dot(a, b, preferred_element_type=F32)


def mm_t(a, b):
    return lax.dot_general(a, b, (((1,), (1,)), ((), ())), preferred_element_type=F32)


def tower(x, w1, w2):
    pre = mm(x, w1)
    sig = 0.5 + 0.5 * jnp.tanh(0.5 * pre)
    out = mm((pre * sig).astype(BF16), w2)
    inv = lax.rsqrt(jnp.sum(out * out, axis=-1, keepdims=True) + NORM_EPS)
    return pre, sig, inv, out * inv


def upright(row):
    return jnp.transpose(jnp.broadcast_to(row, (128, row.shape[1])))


def spread(at, grads):
    half = 2048
    low = jnp.where(at >= half, at - half, at)
    hot = jnp.where(
        lax.broadcasted_iota(jnp.int32, (half, at.shape[1]), 0) == low, 1.0, 0.0
    ).astype(BF16)
    upper = upright(at.astype(F32)) >= half
    grads = grads.astype(F32)
    both = jnp.concatenate(
        [jnp.where(upper, 0.0, grads), jnp.where(upper, grads, 0.0)], axis=1
    ).astype(BF16)
    return mm(hot, both)


def window_kernel(
    pos_slot, neg_slot, lists, id_rows, counts, table, w1, w2, u1, u2, pos_at, neg_at, user_table,
    d_out, slopes, loss,
    ut, low, high, plow, phigh, unit, wide, send, recv, cols, group, pexp, nexp, scaled,
    sums_out, sums_in, rates, acc, back_send, back_recv, live_rows, rows, row_at,
    ids, meet, t_sem, i_sem, u_sem, o_sem, a_send, a_recv, b_send, b_recv, l_sem,
    q_send, q_recv, f_send, f_recv, s_send, s_recv, r_send, r_recv,
):
    n, users = table.shape[0], group.shape[1]
    cap = 32
    grp, rep = lax.axis_size("grp"), lax.axis_size("rep")
    peers = grp * rep
    chips = grp // 2
    g, r = lax.axis_index("grp"), lax.axis_index("rep")
    me = g * rep + r
    chip, core = g // 2, lax.rem(g, 2)

    def place(t):
        return (t // rep, lax.rem(t, rep))

    barrier = pltpu.get_barrier_semaphore()

    def greet(sem, to):
        pl.semaphore_signal(sem, inc=1, device_id=to, device_id_type=MESH)

    def greet_grp(k, c):
        greet(barrier, (lax.rem(g + k, grp), r))
        return c

    def greet_rep(k, c):
        greet(barrier, (g, lax.rem(r + k, rep)))
        return c

    def greet_again(k, c):
        greet(meet, (g, lax.rem(r + k, rep)))
        return c

    lax.fori_loop(1, grp, greet_grp, 0)
    lax.fori_loop(1, rep, greet_rep, 0)
    fetch = pltpu.make_async_copy(user_table, ut, t_sem)
    fetch.start()

    live = lax.broadcasted_iota(jnp.int32, lists.shape, 0) < counts[...]
    live_rows[...] = jnp.where(live, lists[...], n)
    index = pltpu.make_async_copy(live_rows, rows, i_sem)
    index.start()
    feat = id_rows.shape[0]
    u_copies = [
        pltpu.make_async_copy(id_rows.at[f], ids.at[pl.ds(f * users, users)], u_sem.at[f])
        for f in range(feat)
    ]
    for c in u_copies:
        c.start()

    unit[pl.ds(n, 8), :] = jnp.zeros((8, unit.shape[1]), F32)

    o_copies = []
    for i in range(n // TILE):
        at = pl.ds(i * TILE, TILE)
        pre, sig, inv, unit[at, :] = tower(table[at, :], w1[...], w2[...])
        pexp[i, :, :512] = (sig * (1.0 + pre * (1.0 - sig)) * inv).astype(BF16)
        o_copies.append(
            pltpu.make_async_copy(pexp.at[i, :, pl.ds(0, 512)], slopes.at[at, :], o_sem.at[i])
        )
        o_copies[-1].start()

    pl.semaphore_wait(barrier, grp + rep - 2)
    lax.fori_loop(1, rep, greet_again, 0)

    low_part = jnp.transpose(live_rows[...].astype(F32))
    high_part = jnp.floor(low_part * (1.0 / 64.0))
    low_part = low_part - 64.0 * high_part
    width = peers // GROUPS * cap
    tiled = (
        lax.broadcasted_iota(jnp.int32, (cap, width), 0)
        == lax.rem(lax.broadcasted_iota(jnp.int32, (cap, width), 1), cap)
    ).astype(F32).astype(BF16)
    along = 64.0 * mm(high_part.astype(BF16), tiled) + mm(low_part.astype(BF16), tiled)
    mine = lax.rem(
        lax.broadcasted_iota(jnp.int32, along.shape, 0), peers // GROUPS
    ) == lax.broadcasted_iota(jnp.int32, along.shape, 1) // cap
    along = jnp.where(mine, along, 0.0)
    for b in range(GROUPS):
        part = along[b * (peers // GROUPS):(b + 1) * (peers // GROUPS), :]
        row_at[b:b + 1, :] = jnp.sum(part, axis=0, keepdims=True).astype(jnp.int32)


    fetch.wait()

    def widen(i, c):
        at = pl.ds(pl.multiple_of(i * 256, 256), 256)
        low[at, :] = ut[at, :128].astype(F32)
        high[at, :] = ut[at, 128:].astype(F32)
        return c

    lax.fori_loop(0, ut.shape[0] // 256, widen, 0)
    pl.semaphore_wait(meet, rep - 1)

    def span(t):
        return pl.ds(pl.multiple_of(t * cap, cap), cap)

    def gather_list(t):
        for j in range(cap):
            wide[pl.ds(t * cap + j, 1), :] = unit[pl.ds(rows[j, t], 1), :]
        send[span(t), :] = wide[span(t), :].astype(BF16)

    def send_list(k, c):
        t = lax.rem(me + k, peers)
        gather_list(t)
        pltpu.make_async_remote_copy(
            src_ref=send.at[span(t), :], dst_ref=recv.at[span(me), :],
            send_sem=a_send, recv_sem=a_recv, device_id=place(t), device_id_type=MESH,
        ).start()
        return c

    index.wait()
    lax.fori_loop(1, peers, send_list, 0)
    gather_list(me)
    keep = pltpu.make_async_copy(send.at[span(me), :], recv.at[span(me), :], l_sem)
    keep.start()

    for c in u_copies:
        c.wait()

    def pool(i, c):
        for k in range(8):
            b = i * 8 + k
            at = [pl.ds(ids[f * users + b], 1) for f in range(feat)]
            lo = [low[a, :] for a in at]
            hi = [high[a, :] for a in at]
            while len(lo) > 1:
                lo = [x + y for x, y in zip(lo[::2], lo[1::2])]
                hi = [x + y for x, y in zip(hi[::2], hi[1::2])]
            plow[pl.ds(b, 1), :] = lo[0]
            phigh[pl.ds(b, 1), :] = hi[0]
        return c

    far = sorted(range(1, chips), key=lambda k: (min(k, chips - k), k))
    names = [(0, 0), (0, 1)] + [(k, 0) for k in far] + [(k, 1) for k in far]
    slot_of = {name: i for i, name in enumerate(names)}

    def push(src, dst, ss, rs, k, flip):
        to = lax.rem(chip + k, chips) * 2 + (1 - core if flip else core)
        return pltpu.make_async_remote_copy(
            src_ref=src, dst_ref=dst, send_sem=ss, recv_sem=rs,
            device_id=(to, r), device_id_type=MESH,
        )

    quarter = users // PARTS

    def piece(slot, c):
        return group.at[slot, pl.ds(c * quarter, quarter), :]

    middle = 2 if chips == 4 else 0
    near = [k for k in far if k != middle]
    q_copies, f_copies = {}, {}
    for c in range(PARTS):
        f_copies[0, c] = push(piece(0, c), piece(1, c), f_send.at[c], f_recv.at[c], 0, 1)
        for k in far:
            s, at = slot_of[(k, 0)], k * PARTS + c
            src, to = 0, chips - k
            if k == middle:
                src, to = (slot_of[(1, 0)], chips - 1) if c % 2 == 0 else (slot_of[(chips - 1, 0)], 1)
            q_copies[k, c] = push(piece(src, c), piece(s, c), q_send.at[at], q_recv.at[at], to, 0)
            f_copies[k, c] = push(
                piece(s, c), piece(slot_of[(k, 1)], c), f_send.at[at], f_recv.at[at], 0, 1
            )

    def near_on(c):
        for k in near:
            q_copies[k, c].wait_recv()
            f_copies[k, c].start()
        if middle:
            q_copies[middle, c].start()

    def far_on(c):
        if middle:
            q_copies[middle, c].wait_recv()
            f_copies[middle, c].start()

    for c in range(PARTS):
        at = pl.ds(c * quarter, quarter)
        lax.fori_loop(c * (quarter // 8), (c + 1) * (quarter // 8), pool, 0)
        pooled = jnp.concatenate([plow[at, :], phigh[at, :]], axis=1).astype(BF16)
        group[0, at, :] = tower(pooled, u1[...], u2[...])[3].astype(BF16)
        for k in near:
            q_copies[k, c].start()
        f_copies[0, c].start()
        if c > 0:
            near_on(c - 1)
        if c > 1:
            far_on(c - 2)
    near_on(PARTS - 1)
    far_on(PARTS - 2)

    keep.wait()
    others = pl.ds(0, (peers - 1) * cap)
    pltpu.make_async_copy(send.at[others, :], recv.at[others, :], a_recv).wait()
    wide[...] = recv[...].astype(F32)

    def pick(i, c):
        for j in range(32):
            low[pl.ds(i * 32 + j, 1), :] = wide[pl.ds(neg_slot[i * 32 + j], 1), :]
        for j in range(32):
            low[pl.ds(users + i * 32 + j, 1), :] = wide[pl.ds(pos_slot[i * 32 + j], 1), :]
        return c

    lax.fori_loop(0, users // 32, pick, 0)
    cols[...] = low[pl.ds(0, 2 * users), :].astype(BF16)

    far_on(PARTS - 1)
    for c in o_copies:
        c.wait()
    s = mm_t(cols[pl.ds(0, users), :], group[0])
    e = jnp.exp2(s * (LOGIT_SCALE * LOG2E))
    nexp[...] = e.astype(BF16)
    neg_sum = jnp.sum(e, axis=0, keepdims=True)
    s_copies = []

    def compute(first, last):
        def one(k, c):
            s = mm_t(cols[pl.ds(users, users), :], group[k])
            e = jnp.exp2(s * (LOGIT_SCALE * LOG2E))
            pexp[k] = e.astype(BF16)
            sums_out[k] = jnp.sum(e, axis=0, keepdims=True)
            return c

        lax.fori_loop(first, last, one, 0)
        for i in range(first, last):
            k, flip = names[i]
            b = slot_of[((chips - k) % chips, flip)]
            s_copies.append(push(sums_out.at[i], sums_in.at[b], s_send.at[i], s_recv.at[b], k, flip))
            s_copies[-1].start()

    for c in f_copies.values():
        c.wait_recv()
    compute(1, 5)
    compute(5, grp)

    s = mm_t(cols[pl.ds(users, users), :], group[0])
    hit = lax.broadcasted_iota(jnp.int32, s.shape, 0) == lax.broadcasted_iota(jnp.int32, s.shape, 1)
    e = jnp.where(hit, 0.0, jnp.exp2(s * (LOGIT_SCALE * LOG2E)))
    own_score = jnp.sum(jnp.where(hit, s, 0.0), axis=0, keepdims=True) * LOGIT_SCALE
    pexp[0] = e.astype(BF16)
    other = neg_sum + jnp.sum(e, axis=0, keepdims=True)

    for c in s_copies:
        c.wait_recv()

    for k in range(1, grp):
        other = other + sums_in[k]
    total = other + jnp.exp2(own_score * LOG2E)
    loss[...] = jnp.log(total) - own_score
    rate = LOGIT_SCALE / total
    rates[0] = rate
    r_copies = []
    for i in range(1, grp):
        k, flip = names[i]
        b = slot_of[((chips - k) % chips, flip)]
        r_copies.append(push(rates.at[0], rates.at[b], r_send.at[i], r_recv.at[b], k, flip))
        r_copies[-1].start()

    scaled[0] = (group[0].astype(F32) * upright(rate)).astype(BF16)
    acc[...] = spread(neg_at[...], mm(nexp[...], scaled[0]))
    own = group[0].astype(F32) * upright(rate * other)
    for c in r_copies:
        c.wait_recv()

    def scale(k, c):
        scaled[k] = (group[k].astype(F32) * upright(rates[k])).astype(BF16)
        return c

    lax.fori_loop(1, grp, scale, 0)
    grads = mm(pexp[0], scaled[0]) - own
    for k in range(1, grp):
        grads = grads + mm(pexp[k], scaled[k])
    total_grads = acc[...] + spread(pos_at[...], grads)
    half = n // 2
    back_send[pl.ds(0, half), :] = total_grads[:, :128].astype(BF16)
    back_send[pl.ds(half, half), :] = total_grads[:, 128:].astype(BF16)

    per = peers // GROUPS

    def send_back(k, c):
        t = lax.rem(me + k, peers)
        pltpu.make_async_remote_copy(
            src_ref=back_send.at[span(t), :], dst_ref=back_recv.at[span(me), :],
            send_sem=b_send, recv_sem=b_recv.at[me // per], device_id=place(t), device_id_type=MESH,
        ).start()
        return c

    lax.fori_loop(1, peers, send_back, 0)
    keep = pltpu.make_async_copy(
        back_send.at[span(me), :], back_recv.at[span(me), :], b_recv.at[me // per]
    )
    keep.start()

    acc[...] = jnp.zeros(acc.shape, F32)

    def arrive(i, c):
        b = lax.rem(me // per + 2 * GROUPS - 1 - i, GROUPS)
        at = pl.ds(pl.multiple_of(b * (per * cap), per * cap), per * cap)
        pltpu.make_async_copy(back_send.at[at, :], back_recv.at[at, :], b_recv.at[b]).wait()
        acc[...] = acc[...] + spread(row_at[pl.ds(b, 1), :], back_recv[at, :])
        return c

    lax.fori_loop(0, GROUPS, arrive, 0)

    for i in range(n // TILE):
        at = pl.ds(i * TILE, TILE)
        side = i * TILE // half * 128
        grad = acc[pl.ds(i * TILE % half, TILE), side:side + 128]
        u = unit[at, :]
        d_out[at, :] = (grad - u * jnp.sum(u * grad, axis=-1, keepdims=True)).astype(BF16)

    for c in list(q_copies.values()) + list(f_copies.values()) + s_copies + r_copies:
        c.wait_send()
    pltpu.make_async_copy(send.at[others, :], recv.at[others, :], a_send).wait()
    pltpu.make_async_copy(back_send.at[others, :], back_recv.at[others, :], b_send).wait()


def row_kernel(d_out, slopes, w1, w2, loss_in, out, loss):
    loss[...] = loss_in[...]
    d_pre = (mm_t(d_out[...], w2[...]) * slopes[...].astype(F32)).astype(BF16)
    out[...] = mm_t(d_pre, w1[...])


def per_device(
    item_table, send_rows, send_count, pos_slot, neg_slot, user_ids,
    user_table, item_w1, item_w2, user_w1, user_w2,
):
    peers, cap = send_rows.shape[1:]
    slots = peers * cap
    n, users = item_table.shape[0], pos_slot.shape[0]
    vocab, outw = user_table.shape[0], item_w2.shape[1]
    grp = lax.axis_size("grp")
    chips = grp // 2
    neg = neg_slot.reshape(-1)

    dma = pltpu.SemaphoreType.DMA
    vm = pltpu.VMEM
    d_out, slopes, loss = pl.pallas_call(
        window_kernel,
        out_shape=[
            jax.ShapeDtypeStruct((n, outw), BF16),
            jax.ShapeDtypeStruct((n, item_w1.shape[1]), BF16),
            jax.ShapeDtypeStruct((1, users), F32),
        ],
        in_specs=[SMEM] * 2 + [VMEM] * 10 + [ANY],
        out_specs=[VMEM, ANY, VMEM],
        scratch_shapes=[
            vm(user_table.shape, BF16), vm((vocab, 128), F32), vm((vocab, 128), F32),
            vm((users, 128), F32), vm((users, 128), F32),
            vm((n + 8, outw), F32), vm((slots, outw), F32),
            vm((slots, outw), BF16), vm((slots, outw), BF16),
            vm((2 * users, outw), BF16),
            vm((grp, users, outw), BF16), vm((grp, users, users), BF16), vm((users, users), BF16),
            vm((grp, users, outw), BF16),
            vm((grp, 1, users), F32), vm((grp, 1, users), F32), vm((grp, 1, users), F32),
            vm((n // 2, 2 * outw), F32),
            vm((slots, outw), BF16), vm((slots, outw), BF16),
            vm((cap, peers), jnp.int32), pltpu.SMEM((cap, peers), jnp.int32),
            vm((GROUPS, slots // GROUPS), jnp.int32),
            pltpu.SMEM((user_ids.size,), jnp.int32), pltpu.SemaphoreType.REGULAR,
            dma, dma, dma((user_ids.shape[1],)), dma((n // TILE,)), dma, dma, dma, dma((GROUPS,)), dma,
            dma((chips * PARTS,)), dma((chips * PARTS,)), dma((chips * PARTS,)), dma((chips * PARTS,)),
            dma((grp,)), dma((grp,)), dma((grp,)), dma((grp,)),
        ],
        compiler_params=pltpu.CompilerParams(
            collective_id=0, has_side_effects=True, vmem_limit_bytes=60 * 2**20
        ),
        cost_estimate=pl.CostEstimate(flops=2**34, bytes_accessed=2**24, transcendentals=2**24),
        name="window",
    )(
        pos_slot, neg, send_rows[0].T, user_ids.T, send_count, item_table, item_w1, item_w2,
        user_w1, user_w2, pos_slot.reshape(1, -1), neg_slot, user_table,
    )
    block = 1024
    table_grad, loss = pl.pallas_call(
        row_kernel,
        out_shape=[
            jax.ShapeDtypeStruct(item_table.shape, F32),
            jax.ShapeDtypeStruct((1, users), F32),
        ],
        grid=(n // block,),
        in_specs=[
            pl.BlockSpec((block, outw), lambda i: (i, 0)),
            pl.BlockSpec((block, item_w1.shape[1]), lambda i: (i, 0)),
            pl.BlockSpec(item_w1.shape, lambda i: (0, 0)),
            pl.BlockSpec(item_w2.shape, lambda i: (0, 0)),
            pl.BlockSpec((1, users), lambda i: (0, 0)),
        ],
        out_specs=[
            pl.BlockSpec((block, item_table.shape[1]), lambda i: (i, 0)),
            pl.BlockSpec((1, users), lambda i: (0, 0)),
        ],
        compiler_params=pltpu.CompilerParams(vmem_limit_bytes=60 * 2**20),
        name="row_grads",
    )(d_out, slopes, item_w1, item_w2, loss)
    return table_grad, loss.reshape(-1)


def solution(mesh):
    return jax.shard_map(
        per_device,
        mesh=mesh,
        in_specs=(
            P(("grp", "rep"), None),
            P(("grp", "rep"), None, None),
            P(("grp", "rep"), None),
            P(("grp", "rep")),
            P(("grp", "rep"), None),
            P(("grp", "rep"), None),
            P(), P(), P(), P(), P(),
        ),
        out_specs=(P(("grp", "rep"), None), P(("grp", "rep"))),
        check_vma=False,
    )
```
